256 devices in a mesh: ctx: 64 (over y, x, z_hi), dp: 4 (over z_lo, core).
Axes of the slice: x: 4, y: 4, z: 8 (z_hi: 4, z_lo: 2; z = z_hi * 2 + z_lo), core: 2. Of those that a mesh axis runs over, the one named last changes fastest.
Arguments:
- token_ids: int32 [4, 8192], P('dp', 'ctx'), may hold values from 0 to 511
- embedding: bfloat16 [512, 2048], replicated, may hold values from -6 to 6
- in_gate: bfloat16 [4, 8192, 2048], P('dp', 'ctx'), may hold values from -6 to 6
- teacher_gate: bfloat16 [4, 8192, 2048], P('dp', 'ctx'), may hold values from -6 to 6
- student_gate: bfloat16 [4, 8192, 2048], P('dp', 'ctx'), may hold values from -6 to 6
- teacher_filter: bfloat16 [8192, 2048], P('ctx')
- student_filter: bfloat16 [8192, 2048], P('ctx')
Outputs:
- student_out: bfloat16 [4, 8192, 2048], P('dp', 'ctx')
- filter_grad: float32 [8192, 2048], P('ctx')
The draws below stay inside these ranges and needn't reach their ends.
All inputs are finite; a program needn't handle non-finite values.
Results may differ from the reference program's by a relative error of at most 0.022.
Values may be sent and summed in bfloat16 or wider, within the bound.
No kernel may reach another device: no remote copies, remote signals or barrier semaphores. Data moves between devices by JAX's collectives and lax.ppermute only.
A program may use at most 128 MiB of HBM per device.

```python
import math
import jax
import jax.numpy as jnp
import numpy as np
from jax import lax

CHANNEL_WIDTH = 2048
VOCAB = 512
TOK_DEV = 128
SEQUENCE_LENGTH = 8192
SEQS = 4
N_CTX = 64


def filter_taps(key, fast_share, slow_low, slow_high, fast_low, fast_high):
    random_subkey_list = jax.random.split(key, 8)
    chooser = jax.random.uniform(random_subkey_list[0], (CHANNEL_WIDTH,))
    slow_logs = jax.random.uniform(random_subkey_list[1], (CHANNEL_WIDTH,), minval=slow_low, maxval=slow_high)
    fast_logs = jax.random.uniform(random_subkey_list[2], (CHANNEL_WIDTH,), minval=fast_low, maxval=fast_high)
    decay_len = jnp.exp(jnp.where(chooser < fast_share, fast_logs, slow_logs))
    pulse_locations = jax.random.randint(random_subkey_list[3], (3, CHANNEL_WIDTH), 0, SEQUENCE_LENGTH)
    pulse_dropoffs = jax.random.uniform(random_subkey_list[4], (3, CHANNEL_WIDTH), minval=0.5, maxval=0.8)
    shift_amounts = jnp.arange(SEQUENCE_LENGTH, dtype=jnp.int32)[:, None]
    lag_values = shift_amounts.astype(jnp.float32)
    decay_profile = jnp.exp(-lag_values / decay_len[None, :])
    for spike_pulse in range(3):
        decay_profile = decay_profile * jnp.where(shift_amounts >= pulse_locations[spike_pulse][None, :], pulse_dropoffs[spike_pulse][None, :], 1.0)
    jitter_vals = jnp.clip(jax.random.normal(random_subkey_list[5], (SEQUENCE_LENGTH, CHANNEL_WIDTH)), -6.0, 6.0)
    main_part = jitter_vals * decay_profile * jnp.sqrt(2.0 / decay_len)[None, :]
    floor_len = float(SEQUENCE_LENGTH)
    floor_share = jax.random.uniform(random_subkey_list[6], (CHANNEL_WIDTH,), minval=0.05, maxval=0.12)
    floor_noise = jnp.clip(jax.random.normal(random_subkey_list[7], (SEQUENCE_LENGTH, CHANNEL_WIDTH)), -6.0, 6.0)
    floor_part = floor_noise * jnp.exp(-lag_values / floor_len) * jnp.sqrt(2.0 * floor_share / floor_len)[None, :]
    return (main_part + floor_part).astype(jnp.float32)


def draw_teacher_filter(key, part):
    key = jax.random.fold_in(key, 11)
    taps = filter_taps(key, 0.4, math.log(SEQUENCE_LENGTH / 2.0), math.log(4.0 * SEQUENCE_LENGTH), math.log(32.0), math.log(256.0))
    return taps.astype(jnp.bfloat16)


def draw_student_filter(key, part):
    key = jax.random.fold_in(key, 23)
    taps = filter_taps(key, 0.4, math.log(SEQUENCE_LENGTH / 2.0), math.log(4.0 * SEQUENCE_LENGTH), math.log(32.0), math.log(256.0))
    return taps.astype(jnp.bfloat16)


def place_ends(result, key, least, high):
    index_at = [jax.random.randint(jax.random.fold_in(key, axis), (), 0, length) for axis, length in enumerate(result.shape)]
    widest = result.shape.index(max(result.shape))
    next_to = index_at[:widest] + [(index_at[widest] + 1) % result.shape[widest]] + index_at[widest + 1:]
    return result.at[tuple(index_at)].set(least).at[tuple(next_to)].set(high)


def levels(stream_key, extent, shards, least, largest):
    def one(position, shards_of):
        steps = jax.random.uniform(jax.random.fold_in(jax.random.fold_in(stream_key, 6), position), (shards_of,), jnp.float32, least / len(shards), largest / len(shards))
        return jnp.repeat(jnp.exp(steps), extent[position] // shards_of).reshape((-1,) + (1,) * (len(extent) - position - 1))

    gain = one(*shards[0])
    for cut in shards[1:]:
        gain = gain * one(*cut)
    return gain


def cumulative_ranks(number_of, slope):
    portions = [(1 << 20) // math.isqrt(grade ** slope) + 1 for grade in range(1, number_of + 1)]
    spread = 1 + sum(portions) // (1 << 30)
    return np.cumsum(np.array([max(1, weight // spread) for weight in portions]))


def ranked(stream_key, extent, number_of, slope):
    listing = cumulative_ranks(number_of, slope)
    ticket = jax.random.randint(jax.random.fold_in(stream_key, 1), extent, 0, int(listing[number_of - 1]))
    standing = jnp.searchsorted(jnp.asarray(listing, jnp.int32), ticket, side="right")
    return jax.random.permutation(jax.random.fold_in(stream_key, 2), number_of)[standing].astype(jnp.int32)


def gaussian(own_key, shape, width, most, pieces=(), kind=jnp.bfloat16):
    result = jax.random.normal(own_key, shape, jnp.float32) * width
    if len(pieces) > 0:
        result = levels(own_key, shape, pieces, -0.22, 0.18) * result
    return jnp.clip(result, min=-most, max=most).astype(kind)


def setup_inputs(seed: int = 0) -> dict:
    key_list = jax.random.split(jax.random.key(seed), 8)
    return {
        "token_ids": place_ends(ranked(key_list[0], (SEQS, SEQUENCE_LENGTH), VOCAB, 2), jax.random.fold_in(key_list[0], 3), 0, VOCAB - 1).astype(jnp.int32),
        "embedding": gaussian(key_list[1], (VOCAB, CHANNEL_WIDTH), 1.0, 6.0),
        "in_gate": gaussian(key_list[2], (SEQS, SEQUENCE_LENGTH, CHANNEL_WIDTH), 1.0, 6.0, ((0, 4), (1, 64))),
        "teacher_gate": gaussian(key_list[3], (SEQS, SEQUENCE_LENGTH, CHANNEL_WIDTH), 1.0, 6.0, ((0, 4), (1, 64))),
        "student_gate": gaussian(key_list[4], (SEQS, SEQUENCE_LENGTH, CHANNEL_WIDTH), 1.0, 6.0, ((0, 4), (1, 64))),
        "teacher_filter": draw_teacher_filter(jax.random.fold_in(key_list[7], 71), 0),
        "student_filter": draw_student_filter(jax.random.fold_in(key_list[7], 71), 0),
    }


def twiddle_angles(span_len):
    freq_idx = jnp.arange(2 * N_CTX, dtype=jnp.int32)
    positions = jnp.arange(TOK_DEV, dtype=jnp.int32)
    prod = (freq_idx[:, None] * positions[None, :]) % span_len
    return prod.astype(jnp.float32) * (2.0 * math.pi / span_len)


def to_bfloat(values):
    part_re = lax.optimization_barrier(jnp.real(values).astype(jnp.bfloat16)).astype(jnp.float32)
    part_im = lax.optimization_barrier(jnp.imag(values).astype(jnp.bfloat16)).astype(jnp.float32)
    return part_re + 1j * part_im


def forward_spec(signal):
    span_len = 2 * SEQUENCE_LENGTH
    blocks = signal.astype(jnp.float32).reshape(N_CTX, TOK_DEV, -1)
    first = jnp.fft.fft(blocks, n=2 * N_CTX, axis=0)
    first = first * jnp.exp(-1j * twiddle_angles(span_len))[:, :, None]
    first = to_bfloat(first)
    return jnp.fft.fft(first, axis=1)


def inverse_spec(spectrum, rounded):
    span_len = 2 * SEQUENCE_LENGTH
    partial_sum = jnp.fft.ifft(spectrum, axis=1) * TOK_DEV
    partial_sum = partial_sum * jnp.exp(1j * twiddle_angles(span_len))[:, :, None]
    if rounded:
        partial_sum = to_bfloat(partial_sum)
    whole = jnp.fft.ifft(partial_sum, axis=0) * (2.0 * N_CTX / span_len)
    return jnp.real(whole[:N_CTX]).reshape(SEQUENCE_LENGTH, -1).astype(jnp.float32)


def reference(token_ids, embedding, in_gate, teacher_gate, student_gate, teacher_filter, student_filter):
    teacher_spec = forward_spec(teacher_filter)
    student_spec = forward_spec(student_filter)

    def one_sequence(inputs):
        ids_row, gate_in, gate_teach, gate_stud = inputs
        values = embedding[ids_row]
        mixed = (gate_in.astype(jnp.float32) * values.astype(jnp.float32)).astype(jnp.bfloat16)
        mixed_spec = forward_spec(mixed)
        conv_t = inverse_spec(mixed_spec * teacher_spec, True).astype(jnp.bfloat16)
        conv_s = inverse_spec(mixed_spec * student_spec, True).astype(jnp.bfloat16)
        teach = gate_teach.astype(jnp.float32) * conv_t.astype(jnp.float32)
        stud = gate_stud.astype(jnp.float32) * conv_s.astype(jnp.float32)
        grad_out = (gate_stud.astype(jnp.float32) * (stud - teach)).astype(jnp.bfloat16)
        grad_spec = forward_spec(grad_out)
        lag_grad = inverse_spec(grad_spec * jnp.conj(mixed_spec), False)
        return stud.astype(jnp.bfloat16), lag_grad

    student_out, lag_grads = lax.map(one_sequence, (token_ids, in_gate, teacher_gate, student_gate))
    filter_grad = jnp.sum(lag_grads, axis=0) * ((SEQS * SEQUENCE_LENGTH) ** -0.5)
    return student_out, filter_grad
```

```python
import functools
import math

import jax
import jax.numpy as jnp
import numpy as np
from jax import lax
from jax.experimental import pallas as pl
from jax.experimental.pallas import tpu as pltpu
from jax.sharding import PartitionSpec as P

SUB = 8
LANES = 128
CHUNK = 256
MIB = 1 << 20


def tables(blocks, inner):
    span = 2 * blocks * inner
    freq = np.arange(blocks, dtype=np.float64) + 0.5
    pos = np.arange(blocks, dtype=np.float64)
    lane = np.arange(inner, dtype=np.float64)
    angle = 2.0 * np.pi * ((freq[:, None] * pos[None, :]) % (2 * blocks)) / (2 * blocks)
    both = np.stack([np.cos(angle), -np.sin(angle)])
    spread = np.einsum("rka,im->rkiam", both, np.eye(SUB))
    spread = spread.reshape(2, blocks * SUB // CHUNK, CHUNK, blocks * SUB)
    first = spread.transpose(1, 0, 2, 3).reshape(2 * blocks * SUB, blocks * SUB)
    turn = 2.0 * np.pi * (freq[:, None] * lane[None, :]) / span
    turn = np.repeat(np.stack([np.cos(turn), np.sin(turn)]), SUB, axis=1)
    angle = 2.0 * np.pi * ((lane[:, None] * lane[None, :]) % inner) / inner
    cosines, sines = np.cos(angle), np.sin(angle)
    second = np.block([[cosines, -sines], [sines, cosines]])
    bf = jnp.bfloat16
    return (
        jnp.asarray(first, bf),
        jnp.asarray(first.T * (2.0 / span), bf),
        jnp.asarray(turn, jnp.float32),
        jnp.asarray(second, bf),
        jnp.asarray(second.T, bf),
    )


def dot(a, b):
    return jnp.dot(a, b, preferred_element_type=jnp.float32)


def dot_nt(a, b):
    return lax.dot_general(a, b, (((1,), (1,)), ((), ())), preferred_element_type=jnp.float32)


def unit(size):
    rows = lax.broadcasted_iota(jnp.int32, (size, size), 0)
    cols = lax.broadcasted_iota(jnp.int32, (size, size), 1)
    return (rows == cols).astype(jnp.float32).astype(jnp.bfloat16)


def pack_kernel(tok_ref, emb_ref, in_ref, teach_ref, stud_ref, ft_ref, fs_ref, out_ref):
    vocab, width = emb_ref.shape
    toks = tok_ref.shape[1]
    rows = lax.broadcasted_iota(jnp.int32, (vocab, toks), 0)
    one_hot = (rows == tok_ref[...]).astype(jnp.float32).astype(jnp.bfloat16)
    values = lax.dot_general(
        one_hot, emb_ref[...], (((0,), (0,)), ((), ())), preferred_element_type=jnp.float32
    )
    mixed = (in_ref[0].astype(jnp.float32) * values).astype(jnp.bfloat16)
    teacher = lax.axis_index("dp") < lax.axis_size("dp") // 2
    taps = jnp.where(teacher, ft_ref[...], fs_ref[...])
    eye = unit(width)
    parts = [
        dot_nt(eye, x).reshape(width // SUB, SUB, toks)
        for x in (mixed, stud_ref[0], teach_ref[0], taps)
    ]
    out_ref[...] = jnp.concatenate(parts, axis=1).astype(jnp.bfloat16)


def pack(token_ids, embedding, in_gate, teacher_gate, student_gate, teacher_filter, student_filter):
    vocab, channels = embedding.shape
    toks = token_ids.shape[1]
    width = 256
    gate = pl.BlockSpec((1, toks, width), lambda g: (0, 0, g))
    taps = pl.BlockSpec((toks, width), lambda g: (0, g))
    return pl.pallas_call(
        pack_kernel,
        grid=(channels // width,),
        in_specs=[
            pl.BlockSpec((1, toks), lambda g: (0, 0)),
            pl.BlockSpec((vocab, width), lambda g: (0, g)),
            gate,
            gate,
            gate,
            taps,
            taps,
        ],
        out_specs=pl.BlockSpec((width // SUB, 4 * SUB, toks), lambda g: (g, 0, 0)),
        out_shape=jax.ShapeDtypeStruct((channels // SUB, 4 * SUB, toks), jnp.bfloat16),
        compiler_params=pltpu.CompilerParams(vmem_limit_bytes=32 * MIB),
    )(token_ids, embedding, in_gate, teacher_gate, student_gate, teacher_filter, student_filter)


def filter_kernel(
    seqs, blocks, scale, in_ref, t1_ref, t1i_ref, turn_ref, t2_ref, t2i_ref, out_ref,
    x_ref, spec_ref, wave_ref, stud_ref, grad_ref, lag_ref,
):
    bf, f32 = jnp.bfloat16, jnp.float32
    toks = in_ref.shape[2]
    full = blocks * SUB
    chunks = full // CHUNK
    per = CHUNK // SUB

    def source(seq, chunk, part):
        data = in_ref[pl.ds(seq * blocks + chunk * per, per)].astype(f32)
        return data[:, part * SUB:(part + 1) * SUB, :].reshape(CHUNK, toks)

    def lanes(n):
        return pl.ds(n * toks, toks)

    def gather(chunk, carry):
        rows = pl.ds(pl.multiple_of(chunk * CHUNK, CHUNK), CHUNK)
        for d in range(seqs):
            x_ref[rows, lanes(d)] = source(d, chunk, 0).astype(bf)
        for f in range(2):
            x_ref[rows, lanes(seqs + f)] = source(f * (seqs // 2), chunk, 3).astype(bf)
        return carry

    lax.fori_loop(0, chunks, gather, 0)

    def forward(chunk, data, count):
        rows = pl.ds(pl.multiple_of(chunk * 2 * CHUNK, CHUNK), 2 * CHUNK)
        turn = pl.ds(pl.multiple_of(chunk * CHUNK, CHUNK), CHUNK)
        cosines, sines = turn_ref[0, turn, :], turn_ref[1, turn, :]
        out = dot(t1_ref[rows, :], data)
        parts = []
        for n in range(count):
            re = out[:CHUNK, n * toks:(n + 1) * toks]
            im = out[CHUNK:, n * toks:(n + 1) * toks]
            parts.append(
                jnp.concatenate([re * cosines + im * sines, im * cosines - re * sines], axis=1)
                .astype(bf)
            )
        return dot(jnp.concatenate(parts, axis=0), t2_ref[...])

    def back(chunk, prod):
        turn = pl.ds(pl.multiple_of(chunk * CHUNK, CHUNK), CHUNK)
        cosines, sines = turn_ref[0, turn, :], turn_ref[1, turn, :]
        re, im = prod[:, :toks], prod[:, toks:]
        return re * cosines - im * sines, im * cosines + re * sines

    def convolve(chunk, carry):
        rows = pl.ds(pl.multiple_of(chunk * CHUNK, CHUNK), CHUNK)
        upper = pl.ds(pl.multiple_of(chunk * 2 * CHUNK, CHUNK), CHUNK)
        lower = pl.ds(pl.multiple_of(chunk * 2 * CHUNK + CHUNK, CHUNK), CHUNK)
        spec = forward(chunk, x_ref[...], seqs + 2)
        for d in range(seqs):
            spec_ref[d, rows, :] = spec[d * CHUNK:(d + 1) * CHUNK]
        for f in range(2):
            taps = spec[(seqs + f) * CHUNK:(seqs + f + 1) * CHUNK]
            tr, ti = taps[:, :toks], taps[:, toks:]
            prods = []
            for d in range(seqs):
                ur = spec[d * CHUNK:(d + 1) * CHUNK, :toks]
                ui = spec[d * CHUNK:(d + 1) * CHUNK, toks:]
                prods.append(
                    jnp.concatenate([ur * tr - ui * ti, ur * ti + ui * tr], axis=1).astype(bf)
                )
            waves = dot(jnp.concatenate(prods, axis=0), t2i_ref[...])
            for d in range(seqs):
                re, im = back(chunk, waves[d * CHUNK:(d + 1) * CHUNK])
                wave_ref[upper, lanes(f * seqs + d)] = re.astype(bf)
                wave_ref[lower, lanes(f * seqs + d)] = im.astype(bf)
        return carry

    lax.fori_loop(0, chunks, convolve, 0)

    def gate(chunk, carry):
        rows = pl.ds(pl.multiple_of(chunk * CHUNK, CHUNK), CHUNK)
        conv = dot(t1i_ref[rows, :], wave_ref[...])
        conv = conv.astype(bf).astype(f32)
        for d in range(seqs):
            conv_t = conv[:, d * toks:(d + 1) * toks]
            conv_s = conv[:, (seqs + d) * toks:(seqs + d + 1) * toks]
            gate_s = source(d, chunk, 1)
            stud = gate_s * conv_s
            stud_ref[rows, lanes(d)] = stud
            grad = gate_s * (stud - source(d, chunk, 2) * conv_t)
            grad_ref[rows, lanes(d)] = grad.astype(bf)
        return carry

    lax.fori_loop(0, chunks, gate, 0)

    def correlate(chunk, carry):
        rows = pl.ds(pl.multiple_of(chunk * CHUNK, CHUNK), CHUNK)
        upper = pl.ds(pl.multiple_of(chunk * 2 * CHUNK, CHUNK), CHUNK)
        lower = pl.ds(pl.multiple_of(chunk * 2 * CHUNK + CHUNK, CHUNK), CHUNK)
        spec = forward(chunk, grad_ref[...], seqs)
        sum_re = jnp.zeros((CHUNK, toks), f32)
        sum_im = jnp.zeros((CHUNK, toks), f32)
        for d in range(seqs):
            gr = spec[d * CHUNK:(d + 1) * CHUNK, :toks]
            gi = spec[d * CHUNK:(d + 1) * CHUNK, toks:]
            ur, ui = spec_ref[d, rows, :toks], spec_ref[d, rows, toks:]
            sum_re += gr * ur + gi * ui
            sum_im += gi * ur - gr * ui
        total = jnp.concatenate([sum_re, sum_im], axis=1)
        high = total.astype(bf)
        low = (total - high.astype(f32)).astype(bf)
        waves = dot(jnp.concatenate([high, low], axis=0), t2i_ref[...])
        re, im = back(chunk, waves[:CHUNK] + waves[CHUNK:])
        for piece, place in ((re, upper), (im, lower)):
            high = piece.astype(bf)
            lag_ref[place, lanes(0)] = high
            lag_ref[place, lanes(1)] = (piece - high.astype(f32)).astype(bf)
        return carry

    lax.fori_loop(0, chunks, correlate, 0)

    def finish(chunk, carry):
        rows = pl.ds(pl.multiple_of(chunk * CHUNK, CHUNK), CHUNK)
        lags = dot(t1i_ref[rows, :], lag_ref[...])
        lags = ((lags[:, :toks] + lags[:, toks:]) * scale).reshape(per, SUB, toks)
        for d in range(seqs):
            stud = stud_ref[rows, lanes(d)].reshape(per, SUB, toks)
            out_ref[pl.ds(d * blocks + chunk * per, per)] = jnp.concatenate(
                [stud, lags], axis=1
            ).astype(bf)
        return carry

    lax.fori_loop(0, chunks, finish, 0)


def filters(data, seqs, blocks):
    toks = data.shape[2]
    full = blocks * SUB
    scale = float(seqs * blocks * toks) ** -0.5
    bf, f32 = jnp.bfloat16, jnp.float32
    return pl.pallas_call(
        functools.partial(filter_kernel, seqs, blocks, scale),
        out_shape=jax.ShapeDtypeStruct((seqs * blocks, 2 * SUB, toks), bf),
        scratch_shapes=[
            pltpu.VMEM((full, (seqs + 2) * toks), bf),
            pltpu.VMEM((seqs, full, 2 * toks), f32),
            pltpu.VMEM((2 * full, 2 * seqs * toks), bf),
            pltpu.VMEM((full, seqs * toks), f32),
            pltpu.VMEM((full, seqs * toks), bf),
            pltpu.VMEM((2 * full, 2 * toks), bf),
        ],
        compiler_params=pltpu.CompilerParams(vmem_limit_bytes=48 * MIB),
    )(data, *tables(blocks, toks))


def unpack_kernel(in_ref, stud_ref, lag_ref):
    count, _, toks = in_ref.shape
    data = in_ref[...].astype(jnp.float32)
    eye = unit(toks)
    stud = data[:, :SUB, :].reshape(count * SUB, toks).astype(jnp.bfloat16)
    lags = data[:, SUB:, :].reshape(count * SUB, toks).astype(jnp.bfloat16)
    stud_ref[0] = dot_nt(eye, stud).astype(jnp.bfloat16)
    lag_ref[...] = dot_nt(eye, lags)


def unpack(data):
    senders, rows, toks = data.shape
    channels = senders * SUB
    width = 256
    return pl.pallas_call(
        unpack_kernel,
        grid=(channels // width,),
        in_specs=[pl.BlockSpec((width // SUB, rows, toks), lambda g: (g, 0, 0))],
        out_specs=(
            pl.BlockSpec((1, toks, width), lambda g: (0, 0, g)),
            pl.BlockSpec((toks, width), lambda g: (0, g)),
        ),
        out_shape=(
            jax.ShapeDtypeStruct((1, toks, channels), jnp.bfloat16),
            jax.ShapeDtypeStruct((toks, channels), jnp.float32),
        ),
        compiler_params=pltpu.CompilerParams(vmem_limit_bytes=32 * MIB),
    )(data)


def body(*args):
    seqs, blocks = lax.axis_size("dp"), lax.axis_size("ctx")

    def exchange(x):
        return lax.all_to_all(x, ("dp", "ctx"), split_axis=0, concat_axis=0, tiled=True)

    return unpack(exchange(filters(exchange(pack(*args)), seqs, blocks)))


def solution(mesh):
    placed = (
        P("dp", "ctx"),
        P(),
        P("dp", "ctx", None),
        P("dp", "ctx", None),
        P("dp", "ctx", None),
        P("ctx", None),
        P("ctx", None),
    )
    return jax.shard_map(
        body,
        mesh=mesh,
        in_specs=placed,
        out_specs=(P("dp", "ctx", None), P("ctx", None)),
        check_vma=False,
    )
```

```python
import functools
import math

import jax
import jax.numpy as jnp
import numpy as np
from jax import lax
from jax.experimental import pallas as pl
from jax.experimental.pallas import tpu as pltpu
from jax.sharding import PartitionSpec as P

SUB = 8
HALF = 4
MESSAGE = 28
LANES = 128
CHUNK = 256
MIB = 1 << 20


def tables(blocks, inner):
    span = 2 * blocks * inner
    freq = np.arange(blocks, dtype=np.float64) + 0.5
    pos = np.arange(blocks, dtype=np.float64)
    lane = np.arange(inner, dtype=np.float64)
    angle = 2.0 * np.pi * ((freq[:, None] * pos[None, :]) % (2 * blocks)) / (2 * blocks)
    both = np.stack([np.cos(angle), -np.sin(angle)])
    spread = np.einsum("rka,im->rkiam", both, np.eye(SUB))
    spread = spread.reshape(2, blocks * SUB // CHUNK, CHUNK, blocks * SUB)
    first = spread.transpose(1, 0, 2, 3).reshape(2 * blocks * SUB, blocks * SUB)
    turn = 2.0 * np.pi * (freq[:, None] * lane[None, :]) / span
    turn = np.repeat(np.stack([np.cos(turn), np.sin(turn)]), SUB, axis=1)
    angle = 2.0 * np.pi * ((lane[:, None] * lane[None, :]) % inner) / inner
    cosines, sines = np.cos(angle), np.sin(angle)
    second = np.block([[cosines, -sines], [sines, cosines]])
    bf = jnp.bfloat16
    return (
        jnp.asarray(first, bf),
        jnp.asarray(first.T * (2.0 / span), bf),
        jnp.asarray(turn, jnp.float32),
        jnp.asarray(second, bf),
        jnp.asarray(second.T, bf),
    )


def dot(a, b):
    return jnp.dot(a, b, preferred_element_type=jnp.float32)


def dot_nt(a, b):
    return lax.dot_general(a, b, (((1,), (1,)), ((), ())), preferred_element_type=jnp.float32)


def turned(x):
    return x.T.astype(jnp.float32)


def unit(size):
    rows = lax.broadcasted_iota(jnp.int32, (size, size), 0)
    cols = lax.broadcasted_iota(jnp.int32, (size, size), 1)
    return (rows == cols).astype(jnp.float32).astype(jnp.bfloat16)


def half_turn(x):
    return jnp.concatenate([x[:, HALF:], x[:, :HALF]], axis=1)


def halves(upper, lower):
    rows = lax.broadcasted_iota(jnp.int32, upper.shape, 1)
    return jnp.where(rows < HALF, upper, lower)


def pack_kernel(
    width, tok_ref, emb_ref, in_ref, stud_ref, teach_ref, ft_ref, fs_ref, out_ref,
    emb_buf, data_buf, sems,
):
    vocab, channels = emb_ref.shape
    toks = tok_ref.shape[1]
    chunks = channels // width
    pairs = width // (2 * SUB)
    dp = lax.axis_index("dp")
    teacher = dp < lax.axis_size("dp") // 2
    lead = lax.rem(dp, 2) == 0
    even = lax.rem(lax.axis_index("ctx"), 2) == 0

    def copies(chunk, taps):
        cols = pl.ds(chunk * width, width)
        sources = (
            (emb_ref.at[:, cols], emb_buf.at[:, cols]),
            (in_ref.at[0, :, cols], data_buf.at[0, :, cols]),
            (stud_ref.at[0, :, cols], data_buf.at[1, :, cols]),
            (teach_ref.at[0, :, cols], data_buf.at[2, :, cols]),
            (taps.at[:, cols], data_buf.at[3, :, cols]),
        )
        return [
            (src, dst, sems.at[chunk, n]) for n, (src, dst) in enumerate(sources)
        ]

    for chunk in range(chunks):
        for copy in copies(chunk, ft_ref)[:4]:
            pltpu.make_async_copy(*copy).start()

        @pl.when(teacher)
        def _():
            pltpu.make_async_copy(*copies(chunk, ft_ref)[4]).start()

        @pl.when(jnp.logical_not(teacher))
        def _():
            pltpu.make_async_copy(*copies(chunk, fs_ref)[4]).start()

    rows = lax.broadcasted_iota(jnp.int32, (vocab, toks), 0)
    one_hot = (rows == tok_ref[...]).astype(jnp.float32).T.astype(jnp.bfloat16)

    for chunk in range(chunks):
        for copy in copies(chunk, ft_ref):
            pltpu.make_async_copy(*copy).wait()
        cols = pl.ds(chunk * width, width)
        values = dot(one_hot, emb_buf[:, cols])
        mixed = (data_buf[0, :, cols].astype(jnp.float32) * values).astype(jnp.bfloat16)
        parts = [
            turned(x).reshape(pairs, 2, SUB, toks)
            for x in (mixed, data_buf[1, :, cols], data_buf[2, :, cols], data_buf[3, :, cols])
        ]
        place = pl.ds(chunk * pairs * 2 * MESSAGE, pairs * 2 * MESSAGE)

        def store(tiles):
            out_ref[place, :] = (
                jnp.stack(tiles, axis=1).reshape(pairs * 2 * MESSAGE, toks).astype(jnp.bfloat16)
            )

        tap_upper = jnp.where(lead, parts[3][:, 0], half_turn(parts[3][:, 0]))
        tap_lower = jnp.where(lead, half_turn(parts[3][:, 1]), parts[3][:, 1])

        @pl.when(even)
        def _():
            mix, stud, teach = [half_turn(x[:, 1]) for x in parts[:3]]
            store([x[:, 0] for x in parts[:3]] + [
                halves(tap_upper, mix), halves(mix, stud), halves(stud, teach),
                halves(teach, tap_lower),
            ])

        @pl.when(jnp.logical_not(even))
        def _():
            mix, stud, teach = [half_turn(x[:, 0]) for x in parts[:3]]
            store([
                halves(tap_upper, mix), halves(mix, stud), halves(stud, teach),
                halves(teach, tap_lower),
            ] + [x[:, 1] for x in parts[:3]])


def pack(token_ids, embedding, in_gate, teacher_gate, student_gate, teacher_filter, student_filter):
    vocab, channels = embedding.shape
    toks = token_ids.shape[1]
    width = 512
    here = pl.BlockSpec(memory_space=pl.ANY)
    return pl.pallas_call(
        functools.partial(pack_kernel, width),
        in_specs=[pl.BlockSpec(memory_space=pltpu.VMEM)] + [here] * 6,
        out_specs=pl.BlockSpec(memory_space=pltpu.VMEM),
        out_shape=jax.ShapeDtypeStruct((channels // SUB * MESSAGE, toks), jnp.bfloat16),
        scratch_shapes=[
            pltpu.VMEM((vocab, channels), jnp.bfloat16),
            pltpu.VMEM((4, toks, channels), jnp.bfloat16),
            pltpu.SemaphoreType.DMA((channels // width, 5)),
        ],
        compiler_params=pltpu.CompilerParams(vmem_limit_bytes=60 * MIB),
    )(token_ids, embedding, in_gate, student_gate, teacher_gate, teacher_filter, student_filter)


def filter_kernel(
    seqs, blocks, scale, in_ref, t1_ref, t1i_ref, turn_ref, t2_ref, t2i_ref, out_ref,
    x_ref, spec_ref, wave_ref, stud_ref, grad_ref, lag_ref,
):
    bf, f32 = jnp.bfloat16, jnp.float32
    toks = in_ref.shape[1]
    full = blocks * SUB
    chunks = full // CHUNK
    per = CHUNK // SUB

    def received(seq, chunk):
        place = pl.multiple_of((seq * blocks + chunk * per) * MESSAGE, per * MESSAGE)
        data = in_ref[pl.ds(place, per * MESSAGE), :].astype(f32)
        return data.reshape(per // 2, 2 * MESSAGE // SUB, SUB, toks)

    def source(data, part):
        return jnp.stack([data[:, part], data[:, part + HALF]], axis=1).reshape(CHUNK, toks)

    def lanes(n):
        return pl.ds(n * toks, toks)

    def gather(chunk, carry):
        rows = pl.ds(pl.multiple_of(chunk * CHUNK, CHUNK), CHUNK)
        taps = []
        for d in range(seqs):
            data = received(d, chunk)
            x_ref[rows, lanes(d)] = source(data, 0).astype(bf)
            taps.append(data[:, HALF - 1])
        for f in range(2):
            lead, other = taps[2 * f:2 * f + 2]
            tile = jnp.stack(
                [halves(lead, half_turn(other)), halves(half_turn(lead), other)], axis=1
            )
            x_ref[rows, lanes(seqs + f)] = tile.reshape(CHUNK, toks).astype(bf)
        return carry

    lax.fori_loop(0, chunks, gather, 0)

    def forward(chunk, data, count):
        rows = pl.ds(pl.multiple_of(chunk * 2 * CHUNK, CHUNK), 2 * CHUNK)
        turn = pl.ds(pl.multiple_of(chunk * CHUNK, CHUNK), CHUNK)
        cosines, sines = turn_ref[0, turn, :], turn_ref[1, turn, :]
        out = dot(t1_ref[rows, :], data)
        parts = []
        for n in range(count):
            re = out[:CHUNK, n * toks:(n + 1) * toks]
            im = out[CHUNK:, n * toks:(n + 1) * toks]
            parts.append(
                jnp.concatenate([re * cosines + im * sines, im * cosines - re * sines], axis=1)
                .astype(bf)
            )
        return dot(jnp.concatenate(parts, axis=0), t2_ref[...])

    def back(chunk, prod):
        turn = pl.ds(pl.multiple_of(chunk * CHUNK, CHUNK), CHUNK)
        cosines, sines = turn_ref[0, turn, :], turn_ref[1, turn, :]
        re, im = prod[:, :toks], prod[:, toks:]
        return re * cosines - im * sines, im * cosines + re * sines

    def convolve(chunk, carry):
        rows = pl.ds(pl.multiple_of(chunk * CHUNK, CHUNK), CHUNK)
        upper = pl.ds(pl.multiple_of(chunk * 2 * CHUNK, CHUNK), CHUNK)
        lower = pl.ds(pl.multiple_of(chunk * 2 * CHUNK + CHUNK, CHUNK), CHUNK)
        spec = forward(chunk, x_ref[...], seqs + 2)
        for d in range(seqs):
            spec_ref[d, rows, :] = spec[d * CHUNK:(d + 1) * CHUNK]
        for f in range(2):
            taps = spec[(seqs + f) * CHUNK:(seqs + f + 1) * CHUNK]
            tr, ti = taps[:, :toks], taps[:, toks:]
            prods = []
            for d in range(seqs):
                ur = spec[d * CHUNK:(d + 1) * CHUNK, :toks]
                ui = spec[d * CHUNK:(d + 1) * CHUNK, toks:]
                prods.append(
                    jnp.concatenate([ur * tr - ui * ti, ur * ti + ui * tr], axis=1).astype(bf)
                )
            waves = dot(jnp.concatenate(prods, axis=0), t2i_ref[...])
            for d in range(seqs):
                re, im = back(chunk, waves[d * CHUNK:(d + 1) * CHUNK])
                wave_ref[upper, lanes(f * seqs + d)] = re.astype(bf)
                wave_ref[lower, lanes(f * seqs + d)] = im.astype(bf)
        return carry

    lax.fori_loop(0, chunks, convolve, 0)

    def gate(chunk, carry):
        rows = pl.ds(pl.multiple_of(chunk * CHUNK, CHUNK), CHUNK)
        conv = dot(t1i_ref[rows, :], wave_ref[...])
        conv = conv.astype(bf).astype(f32)
        for d in range(seqs):
            conv_t = conv[:, d * toks:(d + 1) * toks]
            conv_s = conv[:, (seqs + d) * toks:(seqs + d + 1) * toks]
            data = received(d, chunk)
            gate_s = source(data, 1)
            stud = gate_s * conv_s
            stud_ref[rows, lanes(d)] = stud
            grad = gate_s * (stud - source(data, 2) * conv_t)
            grad_ref[rows, lanes(d)] = grad.astype(bf)
        return carry

    lax.fori_loop(0, chunks, gate, 0)

    def correlate(chunk, carry):
        rows = pl.ds(pl.multiple_of(chunk * CHUNK, CHUNK), CHUNK)
        upper = pl.ds(pl.multiple_of(chunk * 2 * CHUNK, CHUNK), CHUNK)
        lower = pl.ds(pl.multiple_of(chunk * 2 * CHUNK + CHUNK, CHUNK), CHUNK)
        spec = forward(chunk, grad_ref[...], seqs)
        sum_re = jnp.zeros((CHUNK, toks), f32)
        sum_im = jnp.zeros((CHUNK, toks), f32)
        for d in range(seqs):
            gr = spec[d * CHUNK:(d + 1) * CHUNK, :toks]
            gi = spec[d * CHUNK:(d + 1) * CHUNK, toks:]
            ur, ui = spec_ref[d, rows, :toks], spec_ref[d, rows, toks:]
            sum_re += gr * ur + gi * ui
            sum_im += gi * ur - gr * ui
        total = jnp.concatenate([sum_re, sum_im], axis=1)
        high = total.astype(bf)
        low = (total - high.astype(f32)).astype(bf)
        waves = dot(jnp.concatenate([high, low], axis=0), t2i_ref[...])
        re, im = back(chunk, waves[:CHUNK] + waves[CHUNK:])
        for piece, place in ((re, upper), (im, lower)):
            high = piece.astype(bf)
            lag_ref[place, lanes(0)] = high
            lag_ref[place, lanes(1)] = (piece - high.astype(f32)).astype(bf)
        return carry

    lax.fori_loop(0, chunks, correlate, 0)

    def finish(chunk, carry):
        rows = pl.ds(pl.multiple_of(chunk * CHUNK, CHUNK), CHUNK)
        lags = dot(t1i_ref[rows, :], lag_ref[...])
        lags = ((lags[:, :toks] + lags[:, toks:]) * scale).reshape(per, SUB, toks)
        for d in range(seqs):
            stud = stud_ref[rows, lanes(d)].reshape(per, SUB, toks)
            out_ref[pl.ds(d * blocks + chunk * per, per)] = jnp.concatenate(
                [stud, lags], axis=1
            ).astype(bf)
        return carry

    lax.fori_loop(0, chunks, finish, 0)


def filters(data, seqs, blocks):
    toks = data.shape[1]
    full = blocks * SUB
    scale = float(seqs * blocks * toks) ** -0.5
    bf, f32 = jnp.bfloat16, jnp.float32
    return pl.pallas_call(
        functools.partial(filter_kernel, seqs, blocks, scale),
        out_shape=jax.ShapeDtypeStruct((seqs * blocks, 2 * SUB, toks), bf),
        scratch_shapes=[
            pltpu.VMEM((full, (seqs + 2) * toks), bf),
            pltpu.VMEM((seqs, full, 2 * toks), f32),
            pltpu.VMEM((2 * full, 2 * seqs * toks), bf),
            pltpu.VMEM((full, seqs * toks), f32),
            pltpu.VMEM((full, seqs * toks), bf),
            pltpu.VMEM((2 * full, 2 * toks), bf),
        ],
        compiler_params=pltpu.CompilerParams(vmem_limit_bytes=48 * MIB),
    )(data, *tables(blocks, toks))


def unpack_kernel(in_ref, stud_ref, lag_ref):
    count, _, toks = in_ref.shape
    data = in_ref[...].astype(jnp.float32)
    eye = unit(toks)
    stud = data[:, :SUB, :].reshape(count * SUB, toks).astype(jnp.bfloat16)
    lags = data[:, SUB:, :].reshape(count * SUB, toks).astype(jnp.bfloat16)
    stud_ref[0] = dot_nt(eye, stud).astype(jnp.bfloat16)
    lag_ref[...] = dot_nt(eye, lags)


def unpack(data):
    senders, rows, toks = data.shape
    channels = senders * SUB
    width = 512
    return pl.pallas_call(
        unpack_kernel,
        grid=(channels // width,),
        in_specs=[pl.BlockSpec((width // SUB, rows, toks), lambda g: (g, 0, 0))],
        out_specs=(
            pl.BlockSpec((1, toks, width), lambda g: (0, 0, g)),
            pl.BlockSpec((toks, width), lambda g: (0, g)),
        ),
        out_shape=(
            jax.ShapeDtypeStruct((1, toks, channels), jnp.bfloat16),
            jax.ShapeDtypeStruct((toks, channels), jnp.float32),
        ),
        compiler_params=pltpu.CompilerParams(vmem_limit_bytes=32 * MIB),
    )(data)


def body(*args):
    seqs, blocks = lax.axis_size("dp"), lax.axis_size("ctx")

    def exchange(x):
        return lax.all_to_all(x, ("dp", "ctx"), split_axis=0, concat_axis=0, tiled=True)

    sent = pack(*args)
    toks = sent.shape[1]
    got = exchange(sent.reshape(seqs * blocks, MESSAGE // HALF, HALF, toks))
    return unpack(exchange(filters(got.reshape(sent.shape), seqs, blocks)))


def solution(mesh):
    placed = (
        P("dp", "ctx"),
        P(),
        P("dp", "ctx", None),
        P("dp", "ctx", None),
        P("dp", "ctx", None),
        P("ctx", None),
        P("ctx", None),
    )
    return jax.shard_map(
        body,
        mesh=mesh,
        in_specs=placed,
        out_specs=(P("dp", "ctx", None), P("ctx", None)),
        check_vma=False,
    )
```

```python
import functools
import math

import jax
import jax.numpy as jnp
import numpy as np
from jax import lax
from jax.experimental import pallas as pl
from jax.experimental.pallas import tpu as pltpu
from jax.sharding import PartitionSpec as P

SUB = 8
HALF = 4
MESSAGE = 28
REPLY = 12
LANES = 128
CHUNK = 512
MIB = 1 << 20


def tables(blocks, inner):
    span = 2 * blocks * inner
    freq = np.arange(blocks, dtype=np.float64) + 0.5
    pos = np.arange(blocks, dtype=np.float64)
    lane = np.arange(inner, dtype=np.float64)
    angle = 2.0 * np.pi * ((freq[:, None] * pos[None, :]) % (2 * blocks)) / (2 * blocks)
    both = np.stack([np.cos(angle), -np.sin(angle)])
    spread = np.einsum("rka,im->rkiam", both, np.eye(SUB))
    spread = spread.reshape(2, blocks * SUB // CHUNK, CHUNK, blocks * SUB)
    first = spread.transpose(1, 0, 2, 3).reshape(2 * blocks * SUB, blocks * SUB)
    turn = 2.0 * np.pi * (freq[:, None] * lane[None, :]) / span
    turn = np.repeat(np.stack([np.cos(turn), np.sin(turn)]), SUB, axis=1)
    angle = 2.0 * np.pi * ((lane[:, None] * lane[None, :]) % inner) / inner
    cosines, sines = np.cos(angle), np.sin(angle)
    second = np.block([[cosines, -sines], [sines, cosines]])
    bf = jnp.bfloat16
    return (
        jnp.asarray(first, bf),
        jnp.asarray(first.T * (2.0 / span), bf),
        jnp.asarray(turn, jnp.float32),
        jnp.asarray(second, bf),
        jnp.asarray(second.T, bf),
    )


def dot(a, b):
    return jnp.dot(a, b, preferred_element_type=jnp.float32)


def turned(x):
    return x.T.astype(jnp.float32)


def half_turn(x):
    return jnp.concatenate([x[:, HALF:], x[:, :HALF]], axis=1)


def halves(upper, lower):
    rows = lax.broadcasted_iota(jnp.int32, upper.shape, 1)
    return jnp.where(rows < HALF, upper, lower)


def pack_kernel(
    width, tok_ref, emb_ref, in_ref, stud_ref, teach_ref, ft_ref, fs_ref, out_ref,
    emb_buf, data_buf, out_buf, sems, out_sems,
):
    vocab, channels = emb_ref.shape
    toks = tok_ref.shape[1]
    chunks = channels // width
    pairs = width // (2 * SUB)
    dp = lax.axis_index("dp")
    teacher = dp < lax.axis_size("dp") // 2
    lead = lax.rem(dp, 2) == 0
    even = lax.rem(lax.axis_index("ctx"), 2) == 0

    def copies(chunk, taps):
        cols = pl.ds(chunk * width, width)
        sources = (
            (emb_ref.at[:, cols], emb_buf.at[:, cols]),
            (in_ref.at[0, :, cols], data_buf.at[0, :, cols]),
            (stud_ref.at[0, :, cols], data_buf.at[1, :, cols]),
            (teach_ref.at[0, :, cols], data_buf.at[2, :, cols]),
            (taps.at[:, cols], data_buf.at[3, :, cols]),
        )
        return [
            (src, dst, sems.at[chunk, n]) for n, (src, dst) in enumerate(sources)
        ]

    for chunk in range(chunks):
        for copy in copies(chunk, ft_ref)[:4]:
            pltpu.make_async_copy(*copy).start()

        @pl.when(teacher)
        def _():
            pltpu.make_async_copy(*copies(chunk, ft_ref)[4]).start()

        @pl.when(jnp.logical_not(teacher))
        def _():
            pltpu.make_async_copy(*copies(chunk, fs_ref)[4]).start()

    rows = lax.broadcasted_iota(jnp.int32, (vocab, toks), 0)
    one_hot = (rows == tok_ref[...]).astype(jnp.float32).T.astype(jnp.bfloat16)

    for chunk in range(chunks):
        for copy in copies(chunk, ft_ref):
            pltpu.make_async_copy(*copy).wait()
        cols = pl.ds(chunk * width, width)
        values = dot(one_hot, emb_buf[:, cols])
        mixed = (data_buf[0, :, cols].astype(jnp.float32) * values).astype(jnp.bfloat16)
        parts = [
            turned(x).reshape(pairs, 2, SUB, toks)
            for x in (mixed, data_buf[1, :, cols], data_buf[2, :, cols], data_buf[3, :, cols])
        ]
        place = pl.ds(chunk * pairs * 2 * MESSAGE, pairs * 2 * MESSAGE)

        def store(tiles):
            out_buf[place, :] = (
                jnp.stack(tiles, axis=1).reshape(pairs * 2 * MESSAGE, toks).astype(jnp.bfloat16)
            )

        tap_upper = jnp.where(lead, parts[3][:, 0], half_turn(parts[3][:, 0]))
        tap_lower = jnp.where(lead, half_turn(parts[3][:, 1]), parts[3][:, 1])

        @pl.when(even)
        def _():
            mix, stud, teach = [half_turn(x[:, 1]) for x in parts[:3]]
            store([x[:, 0] for x in parts[:3]] + [
                halves(tap_upper, mix), halves(mix, stud), halves(stud, teach),
                halves(teach, tap_lower),
            ])

        @pl.when(jnp.logical_not(even))
        def _():
            mix, stud, teach = [half_turn(x[:, 0]) for x in parts[:3]]
            store([
                halves(tap_upper, mix), halves(mix, stud), halves(stud, teach),
                halves(teach, tap_lower),
            ] + [x[:, 1] for x in parts[:3]])

        pltpu.make_async_copy(
            out_buf.at[place, :], out_ref.at[place, :], out_sems.at[chunk]
        ).start()

    for chunk in range(chunks):
        place = pl.ds(chunk * pairs * 2 * MESSAGE, pairs * 2 * MESSAGE)
        pltpu.make_async_copy(
            out_buf.at[place, :], out_ref.at[place, :], out_sems.at[chunk]
        ).wait()


def pack(token_ids, embedding, in_gate, teacher_gate, student_gate, teacher_filter, student_filter):
    vocab, channels = embedding.shape
    toks = token_ids.shape[1]
    width = 512
    here = pl.BlockSpec(memory_space=pl.ANY)
    return pl.pallas_call(
        functools.partial(pack_kernel, width),
        in_specs=[pl.BlockSpec(memory_space=pltpu.VMEM)] + [here] * 6,
        out_specs=here,
        out_shape=jax.ShapeDtypeStruct((channels // SUB * MESSAGE, toks), jnp.bfloat16),
        scratch_shapes=[
            pltpu.VMEM((vocab, channels), jnp.bfloat16),
            pltpu.VMEM((4, toks, channels), jnp.bfloat16),
            pltpu.VMEM((channels // SUB * MESSAGE, toks), jnp.bfloat16),
            pltpu.SemaphoreType.DMA((channels // width, 5)),
            pltpu.SemaphoreType.DMA((channels // width,)),
        ],
        compiler_params=pltpu.CompilerParams(vmem_limit_bytes=60 * MIB),
    )(token_ids, embedding, in_gate, student_gate, teacher_gate, teacher_filter, student_filter)


def filter_kernel(
    seqs, blocks, scale, in_ref, t1_ref, t1i_ref, turn_ref, t2_ref, t2i_ref, out_ref,
    x_ref, spec_ref, wave_ref, stud_ref, grad_ref, lag_ref,
):
    bf, f32 = jnp.bfloat16, jnp.float32
    toks = in_ref.shape[1]
    full = blocks * SUB
    chunks = full // CHUNK
    per = CHUNK // SUB

    def received(seq, chunk):
        place = pl.multiple_of((seq * blocks + chunk * per) * MESSAGE, per * MESSAGE)
        data = in_ref[pl.ds(place, per * MESSAGE), :].astype(f32)
        return data.reshape(per // 2, 2 * MESSAGE // SUB, SUB, toks)

    def source(data, part):
        return jnp.stack([data[:, part], data[:, part + HALF]], axis=1).reshape(CHUNK, toks)

    def lanes(n):
        return pl.ds(n * toks, toks)

    def gather(chunk, carry):
        rows = pl.ds(pl.multiple_of(chunk * CHUNK, CHUNK), CHUNK)
        taps = []
        for d in range(seqs):
            data = received(d, chunk)
            x_ref[rows, lanes(d)] = source(data, 0).astype(bf)
            taps.append(data[:, HALF - 1])
        for f in range(2):
            lead, other = taps[2 * f:2 * f + 2]
            tile = jnp.stack(
                [halves(lead, half_turn(other)), halves(half_turn(lead), other)], axis=1
            )
            x_ref[rows, lanes(seqs + f)] = tile.reshape(CHUNK, toks).astype(bf)
        return carry

    lax.fori_loop(0, chunks, gather, 0)

    def forward(chunk, data, count):
        rows = pl.ds(pl.multiple_of(chunk * 2 * CHUNK, CHUNK), 2 * CHUNK)
        turn = pl.ds(pl.multiple_of(chunk * CHUNK, CHUNK), CHUNK)
        cosines, sines = turn_ref[0, turn, :], turn_ref[1, turn, :]
        out = dot(t1_ref[rows, :], data)
        parts = []
        for n in range(count):
            re = out[:CHUNK, n * toks:(n + 1) * toks]
            im = out[CHUNK:, n * toks:(n + 1) * toks]
            parts.append(
                jnp.concatenate([re * cosines + im * sines, im * cosines - re * sines], axis=1)
                .astype(bf)
            )
        return dot(jnp.concatenate(parts, axis=0), t2_ref[...])

    def back(chunk, prod):
        turn = pl.ds(pl.multiple_of(chunk * CHUNK, CHUNK), CHUNK)
        cosines, sines = turn_ref[0, turn, :], turn_ref[1, turn, :]
        re, im = prod[:, :toks], prod[:, toks:]
        return re * cosines - im * sines, im * cosines + re * sines

    def convolve(chunk, carry):
        rows = pl.ds(pl.multiple_of(chunk * CHUNK, CHUNK), CHUNK)
        upper = pl.ds(pl.multiple_of(chunk * 2 * CHUNK, CHUNK), CHUNK)
        lower = pl.ds(pl.multiple_of(chunk * 2 * CHUNK + CHUNK, CHUNK), CHUNK)
        spec = forward(chunk, x_ref[...], seqs + 2)
        for d in range(seqs):
            spec_ref[d, rows, :] = spec[d * CHUNK:(d + 1) * CHUNK]
        for f in range(2):
            taps = spec[(seqs + f) * CHUNK:(seqs + f + 1) * CHUNK]
            tr, ti = taps[:, :toks], taps[:, toks:]
            prods = []
            for d in range(seqs):
                ur = spec[d * CHUNK:(d + 1) * CHUNK, :toks]
                ui = spec[d * CHUNK:(d + 1) * CHUNK, toks:]
                prods.append(
                    jnp.concatenate([ur * tr - ui * ti, ur * ti + ui * tr], axis=1).astype(bf)
                )
            waves = dot(jnp.concatenate(prods, axis=0), t2i_ref[...])
            for d in range(seqs):
                re, im = back(chunk, waves[d * CHUNK:(d + 1) * CHUNK])
                wave_ref[upper, lanes(f * seqs + d)] = re.astype(bf)
                wave_ref[lower, lanes(f * seqs + d)] = im.astype(bf)
        return carry

    lax.fori_loop(0, chunks, convolve, 0)

    def gate(chunk, carry):
        rows = pl.ds(pl.multiple_of(chunk * CHUNK, CHUNK), CHUNK)
        conv = dot(t1i_ref[rows, :], wave_ref[...])
        conv = conv.astype(bf).astype(f32)
        for d in range(seqs):
            conv_t = conv[:, d * toks:(d + 1) * toks]
            conv_s = conv[:, (seqs + d) * toks:(seqs + d + 1) * toks]
            data = received(d, chunk)
            gate_s = source(data, 1)
            stud = gate_s * conv_s
            stud_ref[rows, lanes(d)] = stud
            grad = gate_s * (stud - source(data, 2) * conv_t)
            grad_ref[rows, lanes(d)] = grad.astype(bf)
        return carry

    lax.fori_loop(0, chunks, gate, 0)

    def correlate(chunk, carry):
        rows = pl.ds(pl.multiple_of(chunk * CHUNK, CHUNK), CHUNK)
        upper = pl.ds(pl.multiple_of(chunk * 2 * CHUNK, CHUNK), CHUNK)
        lower = pl.ds(pl.multiple_of(chunk * 2 * CHUNK + CHUNK, CHUNK), CHUNK)
        spec = forward(chunk, grad_ref[...], seqs)
        sum_re = jnp.zeros((CHUNK, toks), f32)
        sum_im = jnp.zeros((CHUNK, toks), f32)
        for d in range(seqs):
            gr = spec[d * CHUNK:(d + 1) * CHUNK, :toks]
            gi = spec[d * CHUNK:(d + 1) * CHUNK, toks:]
            ur, ui = spec_ref[d, rows, :toks], spec_ref[d, rows, toks:]
            sum_re += gr * ur + gi * ui
            sum_im += gi * ur - gr * ui
        total = jnp.concatenate([sum_re, sum_im], axis=1)
        high = total.astype(bf)
        low = (total - high.astype(f32)).astype(bf)
        waves = dot(jnp.concatenate([high, low], axis=0), t2i_ref[...])
        re, im = back(chunk, waves[:CHUNK] + waves[CHUNK:])
        for piece, place in ((re, upper), (im, lower)):
            high = piece.astype(bf)
            lag_ref[place, lanes(0)] = high
            lag_ref[place, lanes(1)] = (piece - high.astype(f32)).astype(bf)
        return carry

    lax.fori_loop(0, chunks, correlate, 0)

    def finish(chunk, carry):
        rows = pl.ds(pl.multiple_of(chunk * CHUNK, CHUNK), CHUNK)
        lags = dot(t1i_ref[rows, :], lag_ref[...])
        lags = ((lags[:, :toks] + lags[:, toks:]) * scale).reshape(per // 2, 2, SUB, toks)
        turned_lags = half_turn(lags.reshape(per, SUB, toks)).reshape(lags.shape)
        middle = (
            halves(lags[:, 0], turned_lags[:, 1]),
            halves(turned_lags[:, 0], lags[:, 1]),
        )
        for d in range(seqs):
            stud = stud_ref[rows, lanes(d)].reshape(per // 2, 2, SUB, toks)
            tiles = jnp.stack([stud[:, 0], middle[d % 2], stud[:, 1]], axis=1)
            place = pl.multiple_of((d * blocks + chunk * per) * REPLY, per * REPLY)
            out_ref[pl.ds(place, per * REPLY), :] = tiles.reshape(per * REPLY, toks).astype(bf)
        return carry

    lax.fori_loop(0, chunks, finish, 0)


def filters(data, seqs, blocks):
    toks = data.shape[1]
    full = blocks * SUB
    scale = float(seqs * blocks * toks) ** -0.5
    bf, f32 = jnp.bfloat16, jnp.float32
    return pl.pallas_call(
        functools.partial(filter_kernel, seqs, blocks, scale),
        out_shape=jax.ShapeDtypeStruct((seqs * blocks * REPLY, toks), bf),
        scratch_shapes=[
            pltpu.VMEM((full, (seqs + 2) * toks), bf),
            pltpu.VMEM((seqs, full, 2 * toks), f32),
            pltpu.VMEM((2 * full, 2 * seqs * toks), bf),
            pltpu.VMEM((full, seqs * toks), f32),
            pltpu.VMEM((full, seqs * toks), bf),
            pltpu.VMEM((2 * full, 2 * toks), bf),
        ],
        compiler_params=pltpu.CompilerParams(vmem_limit_bytes=48 * MIB),
    )(data, *tables(blocks, toks))


def unpack_kernel(mine_ref, other_ref, stud_ref, lag_ref):
    rows, toks = mine_ref.shape
    pairs = rows // (2 * REPLY)
    even = lax.rem(lax.axis_index("ctx"), 2) == 0
    lead = lax.rem(lax.axis_index("dp"), 2) == 0

    def tiles(ref):
        data = ref[...].astype(jnp.float32).reshape(pairs, 3, SUB, toks)
        return data[:, 0], data[:, 1], data[:, 2]

    def channels(upper, lower):
        both = jnp.stack([upper, lower], axis=1).reshape(pairs * 2 * SUB, toks)
        return both.astype(jnp.bfloat16).T

    first, middle, last = tiles(mine_ref)
    crossed = half_turn(middle)
    upper = jnp.where(even, first, halves(half_turn(first), crossed))
    lower = jnp.where(even, halves(crossed, half_turn(last)), last)
    stud_ref[0] = channels(upper, lower)

    def taps(first, middle, last):
        return jnp.where(even, halves(middle, last), halves(first, middle))

    mine = taps(first, middle, last)
    other = taps(*tiles(other_ref))
    upper = jnp.where(lead, mine, other)
    lower = jnp.where(lead, other, mine)
    lag_ref[...] = channels(
        halves(upper, half_turn(lower)), halves(half_turn(upper), lower)
    ).astype(jnp.float32)


def unpack(mine, other):
    rows, toks = mine.shape
    channels = rows // REPLY * SUB
    width = 1024
    message = pl.BlockSpec((width // SUB * REPLY, toks), lambda g: (g, 0))
    return pl.pallas_call(
        unpack_kernel,
        grid=(channels // width,),
        in_specs=[message, message],
        out_specs=(
            pl.BlockSpec((1, toks, width), lambda g: (0, 0, g)),
            pl.BlockSpec((toks, width), lambda g: (0, g)),
        ),
        out_shape=(
            jax.ShapeDtypeStruct((1, toks, channels), jnp.bfloat16),
            jax.ShapeDtypeStruct((toks, channels), jnp.float32),
        ),
        compiler_params=pltpu.CompilerParams(vmem_limit_bytes=32 * MIB),
    )(mine, other)


def body(*args):
    seqs, blocks = lax.axis_size("dp"), lax.axis_size("ctx")

    def exchange(x):
        cut = x.reshape(seqs * blocks, -1, HALF, x.shape[1])
        got = lax.all_to_all(cut, ("dp", "ctx"), split_axis=0, concat_axis=0, tiled=True)
        return got.reshape(x.shape)

    got = exchange(filters(exchange(pack(*args)), seqs, blocks))
    partner = [(d, d + 1 - 2 * (d % 2)) for d in range(seqs)]
    return unpack(got, lax.ppermute(got, "dp", partner))


def solution(mesh):
    placed = (
        P("dp", "ctx"),
        P(),
        P("dp", "ctx", None),
        P("dp", "ctx", None),
        P("dp", "ctx", None),
        P("ctx", None),
        P("ctx", None),
    )
    return jax.shard_map(
        body,
        mesh=mesh,
        in_specs=placed,
        out_specs=(P("dp", "ctx", None), P("ctx", None)),
        check_vma=False,
    )
```

```python
import functools

import jax
import jax.numpy as jnp
import numpy as np
from jax import lax
from jax.experimental import pallas as pl
from jax.experimental.pallas import tpu as pltpu
from jax.sharding import PartitionSpec as P

SUB = 8
HALF = 4
MESSAGE = 28
REPLY = 12
MIB = 1 << 20


def tables(blocks, inner):
    span = 2 * blocks * inner
    freq = np.arange(blocks, dtype=np.float64) + 0.5
    pos = np.arange(blocks, dtype=np.float64)
    lane = np.arange(inner, dtype=np.float64)
    angle = 2.0 * np.pi * ((freq[:, None] * pos[None, :]) % (2 * blocks)) / (2 * blocks)
    both = np.stack([np.cos(angle), -np.sin(angle)])
    spread = np.einsum("rka,im->rkiam", both, np.eye(HALF))
    swapped = spread.reshape(2, blocks, HALF, blocks // 2, 2, HALF)[:, :, :, :, ::-1]
    shape = (2 * blocks * HALF, blocks * HALF)
    first = np.stack([spread.reshape(shape), swapped.reshape(shape)])
    turn = 2.0 * np.pi * (freq[:, None] * lane[None, :]) / span
    turn = np.repeat(np.stack([np.cos(turn), np.sin(turn)]), HALF, axis=1)
    turn = np.concatenate([turn, turn], axis=1)
    angle = 2.0 * np.pi * ((lane[:, None] * lane[None, :]) % inner) / inner
    cosines, sines = np.cos(angle), np.sin(angle)
    second = np.block([[cosines, -sines], [sines, cosines]])
    bf = jnp.bfloat16
    return (
        jnp.asarray(first, bf),
        jnp.asarray(first.transpose(0, 2, 1) * (2.0 / span), bf),
        jnp.asarray(turn, jnp.float32),
        jnp.asarray(second, bf),
        jnp.asarray(second.T, bf),
    )


def dot(a, b):
    return jnp.dot(a, b, preferred_element_type=jnp.float32)


def turned(x):
    return x.T.astype(jnp.float32)


def half_turn(x):
    return jnp.concatenate([x[:, HALF:], x[:, :HALF]], axis=1)


def halves(upper, lower):
    rows = lax.broadcasted_iota(jnp.int32, upper.shape, 1)
    return jnp.where(rows < HALF, upper, lower)


def pack_kernel(
    width, tok_ref, emb_ref, in_ref, stud_ref, teach_ref, ft_ref, fs_ref, out_ref,
    emb_buf, data_buf, out_buf, sems, out_sems,
):
    vocab, channels = emb_ref.shape
    toks = tok_ref.shape[1]
    chunks = channels // width
    pairs = width // (2 * SUB)
    dp = lax.axis_index("dp")
    teacher = dp < lax.axis_size("dp") // 2
    lead = lax.rem(dp, 2) == 0
    even = lax.rem(lax.axis_index("ctx"), 2) == 0

    def copies(chunk, taps):
        cols = pl.ds(chunk * width, width)
        sources = (
            (emb_ref.at[:, cols], emb_buf.at[:, cols]),
            (in_ref.at[0, :, cols], data_buf.at[0, :, cols]),
            (stud_ref.at[0, :, cols], data_buf.at[1, :, cols]),
            (teach_ref.at[0, :, cols], data_buf.at[2, :, cols]),
            (taps.at[:, cols], data_buf.at[3, :, cols]),
        )
        return [
            (src, dst, sems.at[chunk, n]) for n, (src, dst) in enumerate(sources)
        ]

    for chunk in range(chunks):
        for copy in copies(chunk, ft_ref)[:4]:
            pltpu.make_async_copy(*copy).start()

        @pl.when(teacher)
        def _():
            pltpu.make_async_copy(*copies(chunk, ft_ref)[4]).start()

        @pl.when(jnp.logical_not(teacher))
        def _():
            pltpu.make_async_copy(*copies(chunk, fs_ref)[4]).start()

    rows = lax.broadcasted_iota(jnp.int32, (vocab, toks), 0)
    one_hot = (rows == tok_ref[...]).astype(jnp.float32).T.astype(jnp.bfloat16)

    for chunk in range(chunks):
        for copy in copies(chunk, ft_ref):
            pltpu.make_async_copy(*copy).wait()
        cols = pl.ds(chunk * width, width)
        values = dot(one_hot, emb_buf[:, cols])
        mixed = (data_buf[0, :, cols].astype(jnp.float32) * values).astype(jnp.bfloat16)
        parts = [
            turned(x).reshape(pairs, 2, SUB, toks)
            for x in (mixed, data_buf[1, :, cols], data_buf[2, :, cols], data_buf[3, :, cols])
        ]
        place = pl.ds(chunk * pairs * 2 * MESSAGE, pairs * 2 * MESSAGE)

        def store(tiles):
            out_buf[place, :] = (
                jnp.stack(tiles, axis=1).reshape(pairs * 2 * MESSAGE, toks).astype(jnp.bfloat16)
            )

        tap_upper = jnp.where(lead, parts[3][:, 0], half_turn(parts[3][:, 0]))
        tap_lower = jnp.where(lead, half_turn(parts[3][:, 1]), parts[3][:, 1])

        @pl.when(even)
        def _():
            mix, stud, teach = [half_turn(x[:, 1]) for x in parts[:3]]
            store([x[:, 0] for x in parts[:3]] + [
                halves(tap_upper, mix), halves(mix, stud), halves(stud, teach),
                halves(teach, tap_lower),
            ])

        @pl.when(jnp.logical_not(even))
        def _():
            mix, stud, teach = [x[:, 0] for x in parts[:3]]
            store([
                halves(tap_upper, mix), halves(mix, stud), halves(stud, teach),
                halves(teach, tap_lower),
            ] + [half_turn(x[:, 1]) for x in parts[:3]])

        pltpu.make_async_copy(
            out_buf.at[place, :], out_ref.at[place, :], out_sems.at[chunk]
        ).start()

    for chunk in range(chunks):
        place = pl.ds(chunk * pairs * 2 * MESSAGE, pairs * 2 * MESSAGE)
        pltpu.make_async_copy(
            out_buf.at[place, :], out_ref.at[place, :], out_sems.at[chunk]
        ).wait()


def pack(token_ids, embedding, in_gate, teacher_gate, student_gate, teacher_filter, student_filter):
    vocab, channels = embedding.shape
    toks = token_ids.shape[1]
    width = 512
    here = pl.BlockSpec(memory_space=pl.ANY)
    return pl.pallas_call(
        functools.partial(pack_kernel, width),
        in_specs=[pl.BlockSpec(memory_space=pltpu.VMEM)] + [here] * 6,
        out_specs=here,
        out_shape=jax.ShapeDtypeStruct((channels // SUB * MESSAGE, toks), jnp.bfloat16),
        scratch_shapes=[
            pltpu.VMEM((vocab, channels), jnp.bfloat16),
            pltpu.VMEM((4, toks, channels), jnp.bfloat16),
            pltpu.VMEM((channels // SUB * MESSAGE, toks), jnp.bfloat16),
            pltpu.SemaphoreType.DMA((channels // width, 5)),
            pltpu.SemaphoreType.DMA((channels // width,)),
        ],
        compiler_params=pltpu.CompilerParams(vmem_limit_bytes=60 * MIB),
    )(token_ids, embedding, in_gate, student_gate, teacher_gate, teacher_filter, student_filter)


def filter_kernel(
    seqs, blocks, scale, in_ref, t1_ref, t1i_ref, turn_ref, t2_ref, t2i_ref, out_ref,
    x_ref, spec_ref, wave_ref, grad_ref, stud_ref, lag_ref,
):
    bf, f32 = jnp.bfloat16, jnp.float32
    toks = in_ref.shape[1]
    full = blocks * SUB
    half = full // 2
    pairs = blocks // 2
    cosines, sines = turn_ref[0], turn_ref[1]

    def received(seq):
        size = blocks * MESSAGE
        data = in_ref[pl.ds(seq * size, size), :].astype(f32)
        return data.reshape(pairs, 2 * MESSAGE // SUB, SUB, toks)

    def sets(data, part):
        even, odd = data[:, part], data[:, part + HALF]
        return jnp.concatenate(
            [halves(even, odd).reshape(half, toks), halves(odd, even).reshape(half, toks)], axis=0
        )

    def lanes(n):
        return pl.ds(n * toks, toks)

    def columns(x, n):
        return x[:, n * toks:(n + 1) * toks]

    for d in range(seqs):
        data = received(d)
        x_ref[:, lanes(d)] = sets(data, 0).astype(bf)
        rows = pl.ds((d % 2) * half, half)
        taps = half_turn(data[:, HALF - 1]) if d % 2 else data[:, HALF - 1]
        x_ref[rows, lanes(seqs + d // 2)] = taps.reshape(half, toks).astype(bf)

    def forward(ref, count):
        outs = [dot(t1_ref[n], ref[pl.ds(n * half, half), :]) for n in range(2)]
        parts = []
        for n in range(count):
            re = jnp.concatenate([columns(out[:half], n) for out in outs], axis=0)
            im = jnp.concatenate([columns(out[half:], n) for out in outs], axis=0)
            parts.append(
                jnp.concatenate([re * cosines + im * sines, im * cosines - re * sines], axis=1)
                .astype(bf)
            )
        return dot(jnp.concatenate(parts, axis=0), t2_ref[...])

    def back(prod):
        re, im = columns(prod, 0), columns(prod, 1)
        return re * cosines - im * sines, im * cosines + re * sines

    def keep(ref, n, re, im):
        ref[pl.ds(0, half), lanes(n)] = re[:half].astype(bf)
        ref[pl.ds(half, half), lanes(n)] = im[:half].astype(bf)
        ref[pl.ds(full, half), lanes(n)] = re[half:].astype(bf)
        ref[pl.ds(full + half, half), lanes(n)] = im[half:].astype(bf)

    def last(ref):
        return [dot(t1i_ref[n], ref[pl.ds(n * full, full), :]) for n in range(2)]

    spec = forward(x_ref, seqs + 2)
    spec_ref[...] = spec[:seqs * full]
    for f in range(2):
        taps = spec[(seqs + f) * full:(seqs + f + 1) * full]
        tr, ti = columns(taps, 0), columns(taps, 1)
        prods = []
        for d in range(seqs):
            ur = columns(spec[d * full:(d + 1) * full], 0)
            ui = columns(spec[d * full:(d + 1) * full], 1)
            prods.append(
                jnp.concatenate([ur * tr - ui * ti, ur * ti + ui * tr], axis=1).astype(bf)
            )
        waves = dot(jnp.concatenate(prods, axis=0), t2i_ref[...])
        for d in range(seqs):
            keep(wave_ref, f * seqs + d, *back(waves[d * full:(d + 1) * full]))

    conv = jnp.concatenate(last(wave_ref), axis=0).astype(bf).astype(f32)
    for d in range(seqs):
        data = received(d)
        gate_s = sets(data, 1)
        stud = gate_s * columns(conv, seqs + d)
        stud_ref[:, lanes(d)] = stud
        grad = gate_s * (stud - sets(data, 2) * columns(conv, d))
        grad_ref[:, lanes(d)] = grad.astype(bf)

    spec = forward(grad_ref, seqs)
    sum_re = jnp.zeros((full, toks), f32)
    sum_im = jnp.zeros((full, toks), f32)
    for d in range(seqs):
        gr = columns(spec[d * full:(d + 1) * full], 0)
        gi = columns(spec[d * full:(d + 1) * full], 1)
        ur = spec_ref[pl.ds(d * full, full), lanes(0)]
        ui = spec_ref[pl.ds(d * full, full), lanes(1)]
        sum_re += gr * ur + gi * ui
        sum_im += gi * ur - gr * ui
    total = jnp.concatenate([sum_re, sum_im], axis=1)
    high = total.astype(bf)
    low = (total - high.astype(f32)).astype(bf)
    waves = dot(jnp.concatenate([high, low], axis=0), t2i_ref[...])
    re, im = back(waves[:full] + waves[full:])
    high_re, high_im = [x.astype(bf).astype(f32) for x in (re, im)]
    keep(lag_ref, 0, high_re, high_im)
    keep(lag_ref, 1, re - high_re, im - high_im)
    lags = [
        ((columns(x, 0) + columns(x, 1)) * scale).reshape(pairs, SUB, toks) for x in last(lag_ref)
    ]
    middle = (lags[0], half_turn(lags[1]))
    for d in range(seqs):
        first = stud_ref[pl.ds(0, half), lanes(d)].reshape(pairs, SUB, toks)
        second = stud_ref[pl.ds(half, half), lanes(d)].reshape(pairs, SUB, toks)
        tiles = jnp.stack([halves(first, second), middle[d % 2], halves(second, first)], axis=1)
        size = blocks * REPLY
        out_ref[pl.ds(d * size, size), :] = tiles.reshape(size, toks).astype(bf)


def filters(data, seqs, blocks):
    toks = data.shape[1]
    full = blocks * SUB
    scale = float(seqs * blocks * toks) ** -0.5
    bf, f32 = jnp.bfloat16, jnp.float32
    return pl.pallas_call(
        functools.partial(filter_kernel, seqs, blocks, scale),
        out_shape=jax.ShapeDtypeStruct((seqs * blocks * REPLY, toks), bf),
        scratch_shapes=[
            pltpu.VMEM((full, (seqs + 2) * toks), bf),
            pltpu.VMEM((seqs * full, 2 * toks), f32),
            pltpu.VMEM((2 * full, 2 * seqs * toks), bf),
            pltpu.VMEM((full, seqs * toks), bf),
            pltpu.VMEM((full, seqs * toks), f32),
            pltpu.VMEM((2 * full, 2 * toks), bf),
        ],
        compiler_params=pltpu.CompilerParams(vmem_limit_bytes=48 * MIB),
    )(data, *tables(blocks, toks))


def tiles(ref):
    rows, toks = ref.shape
    data = ref[...].astype(jnp.float32).reshape(rows // (3 * SUB), 3, SUB, toks)
    return data[:, 0], data[:, 1], data[:, 2]


def channels(upper, lower):
    pairs, _, toks = upper.shape
    both = jnp.stack([upper, lower], axis=1).reshape(pairs * 2 * SUB, toks)
    return both.astype(jnp.bfloat16).T


def student_kernel(in_ref, out_ref):
    even = lax.rem(lax.axis_index("ctx"), 2) == 0
    first, middle, last = tiles(in_ref)
    turned_last = half_turn(last)
    upper = jnp.where(even, first, halves(middle, first))
    lower = jnp.where(even, halves(half_turn(middle), turned_last), turned_last)
    out_ref[0] = channels(upper, lower)


def lags_kernel(mine_ref, other_ref, out_ref):
    even = lax.rem(lax.axis_index("ctx"), 2) == 0
    lead = lax.rem(lax.axis_index("dp"), 2) == 0

    def taps(ref):
        first, middle, last = tiles(ref)
        return jnp.where(even, halves(middle, last), halves(first, middle))

    mine, other = taps(mine_ref), taps(other_ref)
    upper = jnp.where(lead, mine, other)
    lower = jnp.where(lead, other, mine)
    out_ref[...] = channels(
        halves(upper, half_turn(lower)), halves(half_turn(upper), lower)
    ).astype(jnp.float32)


def unpack(mine, other):
    rows, toks = mine.shape
    count = rows // REPLY * SUB
    width = 1024
    message = pl.BlockSpec((width // SUB * REPLY, toks), lambda g: (g, 0))
    params = pltpu.CompilerParams(vmem_limit_bytes=32 * MIB)
    size = pl.CostEstimate(flops=MIB, bytes_accessed=2 * MIB, transcendentals=0)
    student = pl.pallas_call(
        student_kernel,
        grid=(count // width,),
        in_specs=[message],
        out_specs=pl.BlockSpec((1, toks, width), lambda g: (0, 0, g)),
        out_shape=jax.ShapeDtypeStruct((1, toks, count), jnp.bfloat16),
        compiler_params=params,
        cost_estimate=size,
    )(mine)
    lags = pl.pallas_call(
        lags_kernel,
        grid=(count // width,),
        in_specs=[message, message],
        out_specs=pl.BlockSpec((toks, width), lambda g: (0, g)),
        out_shape=jax.ShapeDtypeStruct((toks, count), jnp.float32),
        compiler_params=params,
        cost_estimate=size,
    )(mine, other)
    return student, lags


def body(*args):
    seqs, blocks = lax.axis_size("dp"), lax.axis_size("ctx")

    def exchange(x):
        cut = x.reshape(seqs * blocks, -1, HALF, x.shape[1])
        got = lax.all_to_all(cut, ("dp", "ctx"), split_axis=0, concat_axis=0, tiled=True)
        return got.reshape(x.shape)

    got = exchange(filters(exchange(pack(*args)), seqs, blocks))
    partner = [(d, d + 1 - 2 * (d % 2)) for d in range(seqs)]
    return unpack(got, lax.ppermute(got, "dp", partner))


def solution(mesh):
    placed = (
        P("dp", "ctx"),
        P(),
        P("dp", "ctx", None),
        P("dp", "ctx", None),
        P("dp", "ctx", None),
        P("ctx", None),
        P("ctx", None),
    )
    return jax.shard_map(
        body,
        mesh=mesh,
        in_specs=placed,
        out_specs=(P("dp", "ctx", None), P("ctx", None)),
        check_vma=False,
    )
```

```python
import functools

import jax
import jax.numpy as jnp
import numpy as np
from jax import lax
from jax.experimental import pallas as pl
from jax.experimental.pallas import tpu as pltpu
from jax.sharding import PartitionSpec as P

SUB = 8
HALF = 4
MESSAGE = 28
REPLY = 12
MIB = 1 << 20


def tables(blocks, inner):
    span = 2 * blocks * inner
    freq = np.arange(blocks, dtype=np.float64) + 0.5
    pos = np.arange(blocks, dtype=np.float64)
    lane = np.arange(inner, dtype=np.float64)
    angle = 2.0 * np.pi * ((freq[:, None] * pos[None, :]) % (2 * blocks)) / (2 * blocks)
    both = np.stack([np.cos(angle), -np.sin(angle)])
    spread = np.einsum("rka,im->rkiam", both, np.eye(HALF))
    swapped = spread.reshape(2, blocks, HALF, blocks // 2, 2, HALF)[:, :, :, :, ::-1]
    shape = (2 * blocks * HALF, blocks * HALF)
    first = np.stack([spread.reshape(shape), swapped.reshape(shape)])
    turn = 2.0 * np.pi * (freq[:, None] * lane[None, :]) / span
    turn = np.repeat(np.stack([np.cos(turn), np.sin(turn)]), HALF, axis=1)
    turn = np.concatenate([turn, turn], axis=1)
    angle = 2.0 * np.pi * ((lane[:, None] * lane[None, :]) % inner) / inner
    cosines, sines = np.cos(angle), np.sin(angle)
    second = np.block([[cosines, -sines], [sines, cosines]])
    bf = jnp.bfloat16
    return (
        jnp.asarray(first, bf),
        jnp.asarray(first.transpose(0, 2, 1) * (2.0 / span), bf),
        jnp.asarray(turn, jnp.float32),
        jnp.asarray(second, bf),
        jnp.asarray(second.T, bf),
    )


def dot(a, b):
    return jnp.dot(a, b, preferred_element_type=jnp.float32)


def turned(x):
    return x.T.astype(jnp.float32)


def half_turn(x):
    return jnp.concatenate([x[:, HALF:], x[:, :HALF]], axis=1)


def halves(upper, lower):
    rows = lax.broadcasted_iota(jnp.int32, upper.shape, 1)
    return jnp.where(rows < HALF, upper, lower)


def pack_kernel(
    widths, tok_ref, emb_ref, in_ref, stud_ref, teach_ref, ft_ref, fs_ref, out_ref,
    emb_buf, data_buf, out_buf, sems, out_sems,
):
    vocab, channels = emb_ref.shape
    toks = tok_ref.shape[1]
    chunks = len(widths)
    dp = lax.axis_index("dp")
    teacher = dp < lax.axis_size("dp") // 2
    lead = lax.rem(dp, 2) == 0
    even = lax.rem(lax.axis_index("ctx"), 2) == 0

    def span(chunk):
        return pl.ds(sum(widths[:chunk]) // SUB * MESSAGE, widths[chunk] // SUB * MESSAGE)

    def copies(chunk, taps):
        cols = pl.ds(sum(widths[:chunk]), widths[chunk])
        sources = (
            (emb_ref.at[:, cols], emb_buf.at[:, cols]),
            (in_ref.at[0, :, cols], data_buf.at[0, :, cols]),
            (stud_ref.at[0, :, cols], data_buf.at[1, :, cols]),
            (teach_ref.at[0, :, cols], data_buf.at[2, :, cols]),
            (taps.at[:, cols], data_buf.at[3, :, cols]),
        )
        return [
            (src, dst, sems.at[chunk, n]) for n, (src, dst) in enumerate(sources)
        ]

    for chunk in range(chunks):
        for copy in copies(chunk, ft_ref)[:4]:
            pltpu.make_async_copy(*copy).start()

        @pl.when(teacher)
        def _():
            pltpu.make_async_copy(*copies(chunk, ft_ref)[4]).start()

        @pl.when(jnp.logical_not(teacher))
        def _():
            pltpu.make_async_copy(*copies(chunk, fs_ref)[4]).start()

    rows = lax.broadcasted_iota(jnp.int32, (vocab, toks), 0)
    one_hot = (rows == tok_ref[...]).astype(jnp.float32).T.astype(jnp.bfloat16)

    for chunk in range(chunks):
        for copy in copies(chunk, ft_ref):
            pltpu.make_async_copy(*copy).wait()
        pairs = widths[chunk] // (2 * SUB)
        cols = pl.ds(sum(widths[:chunk]), widths[chunk])
        values = dot(one_hot, emb_buf[:, cols])
        mixed = (data_buf[0, :, cols].astype(jnp.float32) * values).astype(jnp.bfloat16)
        parts = [
            turned(x).reshape(pairs, 2, SUB, toks)
            for x in (mixed, data_buf[1, :, cols], data_buf[2, :, cols], data_buf[3, :, cols])
        ]
        place = span(chunk)

        def store(tiles):
            out_buf[place, :] = (
                jnp.stack(tiles, axis=1).reshape(pairs * 2 * MESSAGE, toks).astype(jnp.bfloat16)
            )

        tap_upper = jnp.where(lead, parts[3][:, 0], half_turn(parts[3][:, 0]))
        tap_lower = jnp.where(lead, half_turn(parts[3][:, 1]), parts[3][:, 1])

        @pl.when(even)
        def _():
            mix, stud, teach = [half_turn(x[:, 1]) for x in parts[:3]]
            store([x[:, 0] for x in parts[:3]] + [
                halves(tap_upper, mix), halves(mix, stud), halves(stud, teach),
                halves(teach, tap_lower),
            ])

        @pl.when(jnp.logical_not(even))
        def _():
            mix, stud, teach = [x[:, 0] for x in parts[:3]]
            store([
                halves(tap_upper, mix), halves(mix, stud), halves(stud, teach),
                halves(teach, tap_lower),
            ] + [half_turn(x[:, 1]) for x in parts[:3]])

        pltpu.make_async_copy(
            out_buf.at[place, :], out_ref.at[place, :], out_sems.at[chunk]
        ).start()

    for chunk in range(chunks):
        place = span(chunk)
        pltpu.make_async_copy(
            out_buf.at[place, :], out_ref.at[place, :], out_sems.at[chunk]
        ).wait()


def pack(token_ids, embedding, in_gate, teacher_gate, student_gate, teacher_filter, student_filter):
    vocab, channels = embedding.shape
    toks = token_ids.shape[1]
    widths = (512,) * (channels // 512)
    here = pl.BlockSpec(memory_space=pl.ANY)
    return pl.pallas_call(
        functools.partial(pack_kernel, widths),
        in_specs=[pl.BlockSpec(memory_space=pltpu.VMEM)] + [here] * 6,
        out_specs=here,
        out_shape=jax.ShapeDtypeStruct((channels // SUB * MESSAGE, toks), jnp.bfloat16),
        scratch_shapes=[
            pltpu.VMEM((vocab, channels), jnp.bfloat16),
            pltpu.VMEM((4, toks, channels), jnp.bfloat16),
            pltpu.VMEM((channels // SUB * MESSAGE, toks), jnp.bfloat16),
            pltpu.SemaphoreType.DMA((len(widths), 5)),
            pltpu.SemaphoreType.DMA((len(widths),)),
        ],
        compiler_params=pltpu.CompilerParams(vmem_limit_bytes=60 * MIB),
    )(token_ids, embedding, in_gate, student_gate, teacher_gate, teacher_filter, student_filter)


def filter_kernel(
    seqs, blocks, scale, in_ref, t1_ref, t1i_ref, turn_ref, t2_ref, t2i_ref, out_ref,
    x_ref, spec_ref, wave_ref, grad_ref, stud_ref, lag_ref,
):
    bf, f32 = jnp.bfloat16, jnp.float32
    toks = in_ref.shape[1]
    full = blocks * SUB
    half = full // 2
    pairs = blocks // 2
    cosines, sines = turn_ref[0], turn_ref[1]

    def received(seq):
        size = blocks * MESSAGE
        data = in_ref[pl.ds(seq * size, size), :].astype(f32)
        return data.reshape(pairs, 2 * MESSAGE // SUB, SUB, toks)

    def sets(data, part):
        even, odd = data[:, part], data[:, part + HALF]
        return jnp.concatenate(
            [halves(even, odd).reshape(half, toks), halves(odd, even).reshape(half, toks)], axis=0
        )

    def lanes(n):
        return pl.ds(n * toks, toks)

    def columns(x, n):
        return x[:, n * toks:(n + 1) * toks]

    for d in range(seqs):
        data = received(d)
        x_ref[:, lanes(d)] = sets(data, 0).astype(bf)
        rows = pl.ds((d % 2) * half, half)
        taps = half_turn(data[:, HALF - 1]) if d % 2 else data[:, HALF - 1]
        x_ref[rows, lanes(seqs + d // 2)] = taps.reshape(half, toks).astype(bf)

    def forward(ref, count):
        outs = [dot(t1_ref[n], ref[pl.ds(n * half, half), :]) for n in range(2)]
        parts = []
        for n in range(count):
            re = jnp.concatenate([columns(out[:half], n) for out in outs], axis=0)
            im = jnp.concatenate([columns(out[half:], n) for out in outs], axis=0)
            parts.append(
                jnp.concatenate([re * cosines + im * sines, im * cosines - re * sines], axis=1)
                .astype(bf)
            )
        return dot(jnp.concatenate(parts, axis=0), t2_ref[...])

    def back(prod):
        re, im = columns(prod, 0), columns(prod, 1)
        return re * cosines - im * sines, im * cosines + re * sines

    def keep(ref, n, re, im):
        ref[pl.ds(0, half), lanes(n)] = re[:half].astype(bf)
        ref[pl.ds(half, half), lanes(n)] = im[:half].astype(bf)
        ref[pl.ds(full, half), lanes(n)] = re[half:].astype(bf)
        ref[pl.ds(full + half, half), lanes(n)] = im[half:].astype(bf)

    def last(ref):
        return [dot(t1i_ref[n], ref[pl.ds(n * full, full), :]) for n in range(2)]

    spec = forward(x_ref, seqs + 2)
    spec_ref[...] = spec[:seqs * full]
    for f in range(2):
        taps = spec[(seqs + f) * full:(seqs + f + 1) * full]
        tr, ti = columns(taps, 0), columns(taps, 1)
        prods = []
        for d in range(seqs):
            ur = columns(spec[d * full:(d + 1) * full], 0)
            ui = columns(spec[d * full:(d + 1) * full], 1)
            prods.append(
                jnp.concatenate([ur * tr - ui * ti, ur * ti + ui * tr], axis=1).astype(bf)
            )
        waves = dot(jnp.concatenate(prods, axis=0), t2i_ref[...])
        for d in range(seqs):
            keep(wave_ref, f * seqs + d, *back(waves[d * full:(d + 1) * full]))

    conv = jnp.concatenate(last(wave_ref), axis=0).astype(bf).astype(f32)
    for d in range(seqs):
        data = received(d)
        gate_s = sets(data, 1)
        stud = gate_s * columns(conv, seqs + d)
        stud_ref[:, lanes(d)] = stud
        grad = gate_s * (stud - sets(data, 2) * columns(conv, d))
        grad_ref[:, lanes(d)] = grad.astype(bf)

    spec = forward(grad_ref, seqs)
    sum_re = jnp.zeros((full, toks), f32)
    sum_im = jnp.zeros((full, toks), f32)
    for d in range(seqs):
        gr = columns(spec[d * full:(d + 1) * full], 0)
        gi = columns(spec[d * full:(d + 1) * full], 1)
        ur = spec_ref[pl.ds(d * full, full), lanes(0)]
        ui = spec_ref[pl.ds(d * full, full), lanes(1)]
        sum_re += gr * ur + gi * ui
        sum_im += gi * ur - gr * ui
    total = jnp.concatenate([sum_re, sum_im], axis=1)
    high = total.astype(bf)
    low = (total - high.astype(f32)).astype(bf)
    waves = dot(jnp.concatenate([high, low], axis=0), t2i_ref[...])
    re, im = back(waves[:full] + waves[full:])
    high_re, high_im = [x.astype(bf).astype(f32) for x in (re, im)]
    keep(lag_ref, 0, high_re, high_im)
    keep(lag_ref, 1, re - high_re, im - high_im)
    lags = [
        ((columns(x, 0) + columns(x, 1)) * scale).reshape(pairs, SUB, toks) for x in last(lag_ref)
    ]
    middle = (lags[0], half_turn(lags[1]))
    for d in range(seqs):
        first = stud_ref[pl.ds(0, half), lanes(d)].reshape(pairs, SUB, toks)
        second = stud_ref[pl.ds(half, half), lanes(d)].reshape(pairs, SUB, toks)
        tiles = jnp.stack([halves(first, second), middle[d % 2], halves(second, first)], axis=1)
        size = blocks * REPLY
        out_ref[pl.ds(d * size, size), :] = tiles.reshape(size, toks).astype(bf)


def filters(data, seqs, blocks):
    toks = data.shape[1]
    full = blocks * SUB
    scale = float(seqs * blocks * toks) ** -0.5
    bf, f32 = jnp.bfloat16, jnp.float32
    return pl.pallas_call(
        functools.partial(filter_kernel, seqs, blocks, scale),
        out_shape=jax.ShapeDtypeStruct((seqs * blocks * REPLY, toks), bf),
        scratch_shapes=[
            pltpu.VMEM((full, (seqs + 2) * toks), bf),
            pltpu.VMEM((seqs * full, 2 * toks), f32),
            pltpu.VMEM((2 * full, 2 * seqs * toks), bf),
            pltpu.VMEM((full, seqs * toks), bf),
            pltpu.VMEM((full, seqs * toks), f32),
            pltpu.VMEM((2 * full, 2 * toks), bf),
        ],
        compiler_params=pltpu.CompilerParams(vmem_limit_bytes=48 * MIB),
    )(data, *tables(blocks, toks))


def tiles(ref):
    rows, toks = ref.shape
    data = ref[...].astype(jnp.float32).reshape(rows // (3 * SUB), 3, SUB, toks)
    return data[:, 0], data[:, 1], data[:, 2]


def channels(upper, lower):
    pairs, _, toks = upper.shape
    both = jnp.stack([upper, lower], axis=1).reshape(pairs * 2 * SUB, toks)
    return both.astype(jnp.bfloat16).T


def student_kernel(in_ref, out_ref):
    even = lax.rem(lax.axis_index("ctx"), 2) == 0
    first, middle, last = tiles(in_ref)
    turned_last = half_turn(last)
    upper = jnp.where(even, first, halves(middle, first))
    lower = jnp.where(even, halves(half_turn(middle), turned_last), turned_last)
    out_ref[0] = channels(upper, lower)


def pick_kernel(in_ref, out_ref):
    even = lax.rem(lax.axis_index("ctx"), 2) == 0
    first, middle, last = tiles(in_ref)
    taps = jnp.where(even, halves(middle, last), halves(first, middle))
    out_ref[...] = taps.reshape(out_ref.shape).astype(jnp.bfloat16)


def lags_kernel(mine_ref, other_ref, out_ref):
    lead = lax.rem(lax.axis_index("dp"), 2) == 0
    rows, toks = mine_ref.shape
    mine, other = [
        ref[...].astype(jnp.float32).reshape(rows // SUB, SUB, toks)
        for ref in (mine_ref, other_ref)
    ]
    upper = jnp.where(lead, mine, other)
    lower = jnp.where(lead, other, mine)
    out_ref[...] = channels(
        halves(upper, half_turn(lower)), halves(half_turn(upper), lower)
    ).astype(jnp.float32)


def unpack(got, swap):
    rows, toks = got.shape
    count = rows // REPLY * SUB
    width = 1024
    message = pl.BlockSpec((width // SUB * REPLY, toks), lambda g: (g, 0))
    picked = pl.BlockSpec((width // 2, toks), lambda g: (g, 0))
    params = pltpu.CompilerParams(vmem_limit_bytes=32 * MIB)
    size = pl.CostEstimate(flops=MIB, bytes_accessed=2 * MIB, transcendentals=0)
    mine = pl.pallas_call(
        pick_kernel,
        out_shape=jax.ShapeDtypeStruct((count // 2, toks), jnp.bfloat16),
        compiler_params=params,
        cost_estimate=size,
    )(got)
    other = swap(mine)
    student = pl.pallas_call(
        student_kernel,
        grid=(count // width,),
        in_specs=[message],
        out_specs=pl.BlockSpec((1, toks, width), lambda g: (0, 0, g)),
        out_shape=jax.ShapeDtypeStruct((1, toks, count), jnp.bfloat16),
        compiler_params=params,
        cost_estimate=size,
    )(got)
    lags = pl.pallas_call(
        lags_kernel,
        grid=(count // width,),
        in_specs=[picked, picked],
        out_specs=pl.BlockSpec((toks, width), lambda g: (0, g)),
        out_shape=jax.ShapeDtypeStruct((toks, count), jnp.float32),
        compiler_params=params,
        cost_estimate=size,
    )(mine, other)
    return student, lags


def body(*args):
    seqs, blocks = lax.axis_size("dp"), lax.axis_size("ctx")

    def exchange(x):
        cut = x.reshape(seqs * blocks, -1, HALF, x.shape[1])
        got = lax.all_to_all(cut, ("dp", "ctx"), split_axis=0, concat_axis=0, tiled=True)
        return got.reshape(x.shape)

    got = exchange(filters(exchange(pack(*args)), seqs, blocks))
    partner = [(d, d + 1 - 2 * (d % 2)) for d in range(seqs)]
    return unpack(got, lambda x: lax.ppermute(x, "dp", partner))


def solution(mesh):
    placed = (
        P("dp", "ctx"),
        P(),
        P("dp", "ctx", None),
        P("dp", "ctx", None),
        P("dp", "ctx", None),
        P("ctx", None),
        P("ctx", None),
    )
    return jax.shard_map(
        body,
        mesh=mesh,
        in_specs=placed,
        out_specs=(P("dp", "ctx", None), P("ctx", None)),
        check_vma=False,
    )
```

```python
import functools

import jax
import jax.numpy as jnp
import numpy as np
from jax import lax
from jax.experimental import pallas as pl
from jax.experimental.pallas import tpu as pltpu
from jax.sharding import PartitionSpec as P

SUB = 8
HALF = 4
MESSAGE = 28
REPLY = 12
MIB = 1 << 20


def tables(blocks, inner):
    span = 2 * blocks * inner
    freq = np.arange(blocks, dtype=np.float64) + 0.5
    pos = np.arange(blocks, dtype=np.float64)
    lane = np.arange(inner, dtype=np.float64)
    angle = 2.0 * np.pi * ((freq[:, None] * pos[None, :]) % (2 * blocks)) / (2 * blocks)
    both = np.stack([np.cos(angle), -np.sin(angle)])
    spread = np.einsum("rka,im->rkiam", both, np.eye(HALF))
    swapped = spread.reshape(2, blocks, HALF, blocks // 2, 2, HALF)[:, :, :, :, ::-1]
    shape = (2 * blocks * HALF, blocks * HALF)
    first = np.stack([spread.reshape(shape), swapped.reshape(shape)])
    turn = 2.0 * np.pi * (freq[:, None] * lane[None, :]) / span
    turn = np.repeat(np.stack([np.cos(turn), np.sin(turn)]), HALF, axis=1)
    turn = np.concatenate([turn, turn], axis=1)
    angle = 2.0 * np.pi * ((lane[:, None] * lane[None, :]) % inner) / inner
    cosines, sines = np.cos(angle), np.sin(angle)
    second = np.block([[cosines, -sines], [sines, cosines]])
    bf = jnp.bfloat16
    return (
        jnp.asarray(first, bf),
        jnp.asarray(first.transpose(0, 2, 1) * (2.0 / span), bf),
        jnp.asarray(turn, jnp.float32),
        jnp.asarray(second, bf),
        jnp.asarray(second.T, bf),
    )


def dot(a, b):
    return jnp.dot(a, b, preferred_element_type=jnp.float32)


def turned(x):
    return x.T.astype(jnp.float32)


def half_turn(x):
    return jnp.concatenate([x[:, HALF:], x[:, :HALF]], axis=1)


def halves(upper, lower):
    rows = lax.broadcasted_iota(jnp.int32, upper.shape, 1)
    return jnp.where(rows < HALF, upper, lower)


def pack_kernel(
    widths, tok_ref, emb_ref, in_ref, stud_ref, teach_ref, ft_ref, fs_ref, out_ref,
    emb_buf, data_buf, out_buf, sems, out_sems,
):
    vocab, channels = emb_ref.shape
    toks = tok_ref.shape[1]
    chunks = len(widths)
    dp = lax.axis_index("dp")
    teacher = dp < lax.axis_size("dp") // 2
    lead = lax.rem(dp, 2) == 0
    even = lax.rem(lax.axis_index("ctx"), 2) == 0

    def span(chunk):
        return pl.ds(sum(widths[:chunk]) // SUB * MESSAGE, widths[chunk] // SUB * MESSAGE)

    def copies(chunk, taps):
        cols = pl.ds(sum(widths[:chunk]), widths[chunk])
        sources = (
            (emb_ref.at[:, cols], emb_buf.at[:, cols]),
            (in_ref.at[0, :, cols], data_buf.at[0, :, cols]),
            (stud_ref.at[0, :, cols], data_buf.at[1, :, cols]),
            (teach_ref.at[0, :, cols], data_buf.at[2, :, cols]),
            (taps.at[:, cols], data_buf.at[3, :, cols]),
        )
        return [
            (src, dst, sems.at[chunk, n]) for n, (src, dst) in enumerate(sources)
        ]

    for chunk in range(chunks):
        for copy in copies(chunk, ft_ref)[:4]:
            pltpu.make_async_copy(*copy).start()

        @pl.when(teacher)
        def _():
            pltpu.make_async_copy(*copies(chunk, ft_ref)[4]).start()

        @pl.when(jnp.logical_not(teacher))
        def _():
            pltpu.make_async_copy(*copies(chunk, fs_ref)[4]).start()

    rows = lax.broadcasted_iota(jnp.int32, (vocab, toks), 0)
    one_hot = (rows == tok_ref[...]).astype(jnp.float32).T.astype(jnp.bfloat16)

    for chunk in range(chunks):
        for copy in copies(chunk, ft_ref):
            pltpu.make_async_copy(*copy).wait()
        pairs = widths[chunk] // (2 * SUB)
        cols = pl.ds(sum(widths[:chunk]), widths[chunk])
        values = dot(one_hot, emb_buf[:, cols])
        mixed = (data_buf[0, :, cols].astype(jnp.float32) * values).astype(jnp.bfloat16)
        parts = [
            turned(x).reshape(pairs, 2, SUB, toks)
            for x in (mixed, data_buf[1, :, cols], data_buf[2, :, cols], data_buf[3, :, cols])
        ]
        place = span(chunk)

        def store(tiles):
            out_buf[place, :] = (
                jnp.stack(tiles, axis=1).reshape(pairs * 2 * MESSAGE, toks).astype(jnp.bfloat16)
            )

        tap_upper = jnp.where(lead, parts[3][:, 0], half_turn(parts[3][:, 0]))
        tap_lower = jnp.where(lead, half_turn(parts[3][:, 1]), parts[3][:, 1])

        @pl.when(even)
        def _():
            mix, stud, teach = [half_turn(x[:, 1]) for x in parts[:3]]
            store([x[:, 0] for x in parts[:3]] + [
                halves(tap_upper, mix), halves(mix, stud), halves(stud, teach),
                halves(teach, tap_lower),
            ])

        @pl.when(jnp.logical_not(even))
        def _():
            mix, stud, teach = [x[:, 0] for x in parts[:3]]
            store([
                halves(tap_upper, mix), halves(mix, stud), halves(stud, teach),
                halves(teach, tap_lower),
            ] + [half_turn(x[:, 1]) for x in parts[:3]])

        pltpu.make_async_copy(
            out_buf.at[place, :], out_ref.at[place, :], out_sems.at[chunk]
        ).start()

    for chunk in range(chunks):
        place = span(chunk)
        pltpu.make_async_copy(
            out_buf.at[place, :], out_ref.at[place, :], out_sems.at[chunk]
        ).wait()


def pack(token_ids, embedding, in_gate, teacher_gate, student_gate, teacher_filter, student_filter):
    vocab, channels = embedding.shape
    toks = token_ids.shape[1]
    widths = (512,) * (channels // 512)
    here = pl.BlockSpec(memory_space=pl.ANY)
    return pl.pallas_call(
        functools.partial(pack_kernel, widths),
        in_specs=[pl.BlockSpec(memory_space=pltpu.VMEM)] + [here] * 6,
        out_specs=here,
        out_shape=jax.ShapeDtypeStruct((channels // SUB * MESSAGE, toks), jnp.bfloat16),
        scratch_shapes=[
            pltpu.VMEM((vocab, channels), jnp.bfloat16),
            pltpu.VMEM((4, toks, channels), jnp.bfloat16),
            pltpu.VMEM((channels // SUB * MESSAGE, toks), jnp.bfloat16),
            pltpu.SemaphoreType.DMA((len(widths), 5)),
            pltpu.SemaphoreType.DMA((len(widths),)),
        ],
        compiler_params=pltpu.CompilerParams(vmem_limit_bytes=60 * MIB),
    )(token_ids, embedding, in_gate, student_gate, teacher_gate, teacher_filter, student_filter)


def filter_kernel(
    seqs, blocks, scale, in_ref, t1_ref, t1i_ref, turn_ref, t2_ref, t2i_ref, out_ref,
    x_ref, spec_ref, wave_ref, grad_ref, stud_ref, lag_ref,
):
    bf, f32 = jnp.bfloat16, jnp.float32
    toks = in_ref.shape[1]
    full = blocks * SUB
    half = full // 2
    pairs = blocks // 2
    cosines, sines = turn_ref[0], turn_ref[1]

    def received(seq):
        size = blocks * MESSAGE
        data = in_ref[pl.ds(seq * size, size), :].astype(f32)
        return data.reshape(pairs, 2 * MESSAGE // SUB, SUB, toks)

    def sets(data, part):
        even, odd = data[:, part], data[:, part + HALF]
        return jnp.concatenate(
            [halves(even, odd).reshape(half, toks), halves(odd, even).reshape(half, toks)], axis=0
        )

    def lanes(n):
        return pl.ds(n * toks, toks)

    def columns(x, n):
        return x[:, n * toks:(n + 1) * toks]

    for d in range(seqs):
        data = received(d)
        x_ref[:, lanes(d)] = sets(data, 0).astype(bf)
        rows = pl.ds((d % 2) * half, half)
        taps = half_turn(data[:, HALF - 1]) if d % 2 else data[:, HALF - 1]
        x_ref[rows, lanes(seqs + d // 2)] = taps.reshape(half, toks).astype(bf)

    def first(ref):
        return [dot(t1_ref[n], ref[pl.ds(n * half, half), :]) for n in range(2)]

    def second(outs, n):
        re = jnp.concatenate([columns(out[:half], n) for out in outs], axis=0)
        im = jnp.concatenate([columns(out[half:], n) for out in outs], axis=0)
        part = jnp.concatenate([re * cosines + im * sines, im * cosines - re * sines], axis=1)
        return dot(part.astype(bf), t2_ref[...])

    def back(prod):
        re, im = columns(prod, 0), columns(prod, 1)
        return re * cosines - im * sines, im * cosines + re * sines

    def keep(ref, n, re, im):
        ref[pl.ds(0, half), lanes(n)] = re[:half].astype(bf)
        ref[pl.ds(half, half), lanes(n)] = im[:half].astype(bf)
        ref[pl.ds(full, half), lanes(n)] = re[half:].astype(bf)
        ref[pl.ds(full + half, half), lanes(n)] = im[half:].astype(bf)

    def last(ref):
        return [dot(t1i_ref[n], ref[pl.ds(n * full, full), :]) for n in range(2)]

    outs = first(x_ref)
    taps = [second(outs, seqs + f) for f in range(2)]
    specs, waves = {}, {}
    for d in range(seqs + 2):
        if d < seqs:
            specs[d] = second(outs, d)
        if 0 <= d - 1 < seqs:
            spec = specs[d - 1]
            spec_ref[pl.ds((d - 1) * full, full), :] = spec
            ur, ui = columns(spec, 0), columns(spec, 1)
            for f in range(2):
                tr, ti = columns(taps[f], 0), columns(taps[f], 1)
                prod = jnp.concatenate([ur * tr - ui * ti, ur * ti + ui * tr], axis=1)
                waves[d - 1, f] = dot(prod.astype(bf), t2i_ref[...])
        if d >= 2:
            for f in range(2):
                keep(wave_ref, 2 * (d - 2) + f, *back(waves[d - 2, f]))

    for d in range(seqs):
        data = received(d)
        gate_s, gate_t = sets(data, 1), sets(data, 2)
        conv = jnp.concatenate(
            [dot(t1i_ref[n], wave_ref[pl.ds(n * full, full), pl.ds(2 * d * toks, 2 * toks)])
             for n in range(2)], axis=0,
        ).astype(bf).astype(f32)
        conv_t, conv_s = columns(conv, 0), columns(conv, 1)
        stud = gate_s * conv_s
        stud_ref[:, lanes(d)] = stud
        grad_ref[:, lanes(d)] = (gate_s * (stud - gate_t * conv_t)).astype(bf)

    outs = first(grad_ref)
    specs = [second(outs, d) for d in range(seqs)]
    sum_re = jnp.zeros((full, toks), f32)
    sum_im = jnp.zeros((full, toks), f32)
    for d in range(seqs):
        gr, gi = columns(specs[d], 0), columns(specs[d], 1)
        ur = spec_ref[pl.ds(d * full, full), lanes(0)]
        ui = spec_ref[pl.ds(d * full, full), lanes(1)]
        sum_re += gr * ur + gi * ui
        sum_im += gi * ur - gr * ui
    total = jnp.concatenate([sum_re, sum_im], axis=1)
    high = total.astype(bf)
    low = (total - high.astype(f32)).astype(bf)
    waves = dot(jnp.concatenate([high, low], axis=0), t2i_ref[...])
    re, im = back(waves[:full] + waves[full:])
    high_re, high_im = [x.astype(bf).astype(f32) for x in (re, im)]
    keep(lag_ref, 0, high_re, high_im)
    keep(lag_ref, 1, re - high_re, im - high_im)
    lags = [
        ((columns(x, 0) + columns(x, 1)) * scale).reshape(pairs, SUB, toks) for x in last(lag_ref)
    ]
    middle = (lags[0], half_turn(lags[1]))
    for d in range(seqs):
        first = stud_ref[pl.ds(0, half), lanes(d)].reshape(pairs, SUB, toks)
        second = stud_ref[pl.ds(half, half), lanes(d)].reshape(pairs, SUB, toks)
        tiles = jnp.stack([halves(first, second), middle[d % 2], halves(second, first)], axis=1)
        size = blocks * REPLY
        out_ref[pl.ds(d * size, size), :] = tiles.reshape(size, toks).astype(bf)


def filters(data, seqs, blocks):
    toks = data.shape[1]
    full = blocks * SUB
    scale = float(seqs * blocks * toks) ** -0.5
    bf, f32 = jnp.bfloat16, jnp.float32
    return pl.pallas_call(
        functools.partial(filter_kernel, seqs, blocks, scale),
        out_shape=jax.ShapeDtypeStruct((seqs * blocks * REPLY, toks), bf),
        scratch_shapes=[
            pltpu.VMEM((full, (seqs + 2) * toks), bf),
            pltpu.VMEM((seqs * full, 2 * toks), f32),
            pltpu.VMEM((2 * full, 2 * seqs * toks), bf),
            pltpu.VMEM((full, seqs * toks), bf),
            pltpu.VMEM((full, seqs * toks), f32),
            pltpu.VMEM((2 * full, 2 * toks), bf),
        ],
        compiler_params=pltpu.CompilerParams(vmem_limit_bytes=48 * MIB),
    )(data, *tables(blocks, toks))


def tiles(ref):
    rows, toks = ref.shape
    data = ref[...].astype(jnp.float32).reshape(rows // (3 * SUB), 3, SUB, toks)
    return data[:, 0], data[:, 1], data[:, 2]


def channels(upper, lower):
    pairs, _, toks = upper.shape
    both = jnp.stack([upper, lower], axis=1).reshape(pairs * 2 * SUB, toks)
    return both.astype(jnp.bfloat16).T


def student_kernel(in_ref, out_ref):
    even = lax.rem(lax.axis_index("ctx"), 2) == 0
    first, middle, last = tiles(in_ref)
    turned_last = half_turn(last)
    upper = jnp.where(even, first, halves(middle, first))
    lower = jnp.where(even, halves(half_turn(middle), turned_last), turned_last)
    out_ref[0] = channels(upper, lower)


def pick_kernel(in_ref, out_ref):
    even = lax.rem(lax.axis_index("ctx"), 2) == 0
    first, middle, last = tiles(in_ref)
    taps = jnp.where(even, halves(middle, last), halves(first, middle))
    out_ref[...] = taps.reshape(out_ref.shape).astype(jnp.bfloat16)


def lags_kernel(mine_ref, other_ref, out_ref):
    lead = lax.rem(lax.axis_index("dp"), 2) == 0
    rows, toks = mine_ref.shape
    mine, other = [
        ref[...].astype(jnp.float32).reshape(rows // SUB, SUB, toks)
        for ref in (mine_ref, other_ref)
    ]
    upper = jnp.where(lead, mine, other)
    lower = jnp.where(lead, other, mine)
    out_ref[...] = channels(
        halves(upper, half_turn(lower)), halves(half_turn(upper), lower)
    ).astype(jnp.float32)


def unpack(got, swap):
    rows, toks = got.shape
    count = rows // REPLY * SUB
    width = 1024
    message = pl.BlockSpec((width // SUB * REPLY, toks), lambda g: (g, 0))
    picked = pl.BlockSpec((width // 2, toks), lambda g: (g, 0))
    params = pltpu.CompilerParams(vmem_limit_bytes=32 * MIB)
    size = pl.CostEstimate(flops=MIB, bytes_accessed=2 * MIB, transcendentals=0)
    mine = pl.pallas_call(
        pick_kernel,
        out_shape=jax.ShapeDtypeStruct((count // 2, toks), jnp.bfloat16),
        compiler_params=params,
        cost_estimate=size,
    )(got)
    other = swap(mine)
    student = pl.pallas_call(
        student_kernel,
        grid=(count // width,),
        in_specs=[message],
        out_specs=pl.BlockSpec((1, toks, width), lambda g: (0, 0, g)),
        out_shape=jax.ShapeDtypeStruct((1, toks, count), jnp.bfloat16),
        compiler_params=params,
        cost_estimate=size,
    )(got)
    lags = pl.pallas_call(
        lags_kernel,
        grid=(count // width,),
        in_specs=[picked, picked],
        out_specs=pl.BlockSpec((toks, width), lambda g: (0, g)),
        out_shape=jax.ShapeDtypeStruct((toks, count), jnp.float32),
        compiler_params=params,
        cost_estimate=size,
    )(mine, other)
    return student, lags


def body(*args):
    seqs, blocks = lax.axis_size("dp"), lax.axis_size("ctx")

    def exchange(x):
        cut = x.reshape(seqs * blocks, -1, HALF, x.shape[1])
        got = lax.all_to_all(cut, ("dp", "ctx"), split_axis=0, concat_axis=0, tiled=True)
        return got.reshape(x.shape)

    got = exchange(filters(exchange(pack(*args)), seqs, blocks))
    partner = [(d, d + 1 - 2 * (d % 2)) for d in range(seqs)]
    return unpack(got, lambda x: lax.ppermute(x, "dp", partner))


def solution(mesh):
    placed = (
        P("dp", "ctx"),
        P(),
        P("dp", "ctx", None),
        P("dp", "ctx", None),
        P("dp", "ctx", None),
        P("ctx", None),
        P("ctx", None),
    )
    return jax.shard_map(
        body,
        mesh=mesh,
        in_specs=placed,
        out_specs=(P("dp", "ctx", None), P("ctx", None)),
        check_vma=False,
    )
```

```python
import functools

import jax
import jax.numpy as jnp
import numpy as np
from jax import lax
from jax.experimental import pallas as pl
from jax.experimental.pallas import tpu as pltpu
from jax.sharding import PartitionSpec as P

SUB = 8
HALF = 4
MESSAGE = 28
REPLY = 12
MIB = 1 << 20


def tables(blocks, inner):
    span = 2 * blocks * inner
    freq = np.arange(blocks, dtype=np.float64) + 0.5
    pos = np.arange(blocks, dtype=np.float64)
    lane = np.arange(inner, dtype=np.float64)
    angle = 2.0 * np.pi * ((freq[:, None] * pos[None, :]) % (2 * blocks)) / (2 * blocks)
    both = np.stack([np.cos(angle), -np.sin(angle)])
    spread = np.einsum("rka,im->rkiam", both, np.eye(HALF))
    swapped = spread.reshape(2, blocks, HALF, blocks // 2, 2, HALF)[:, :, :, :, ::-1]
    shape = (2 * blocks * HALF, blocks * HALF)
    first = np.stack([spread.reshape(shape), swapped.reshape(shape)])
    turn = 2.0 * np.pi * (freq[:, None] * lane[None, :]) / span
    turn = np.repeat(np.stack([np.cos(turn), np.sin(turn)]), HALF, axis=1)
    turn = np.concatenate([turn, turn], axis=1)
    angle = 2.0 * np.pi * ((lane[:, None] * lane[None, :]) % inner) / inner
    cosines, sines = np.cos(angle), np.sin(angle)
    second = np.block([[cosines, -sines], [sines, cosines]])
    bf = jnp.bfloat16
    return (
        jnp.asarray(first, bf),
        jnp.asarray(first.transpose(0, 2, 1) * (2.0 / span), bf),
        jnp.asarray(turn, jnp.float32),
        jnp.asarray(second, bf),
        jnp.asarray(second.T, bf),
    )


def dot(a, b):
    return jnp.dot(a, b, preferred_element_type=jnp.float32)


def turned(x):
    return x.T.astype(jnp.float32)


def half_turn(x):
    return jnp.concatenate([x[:, HALF:], x[:, :HALF]], axis=1)


def halves(upper, lower):
    rows = lax.broadcasted_iota(jnp.int32, upper.shape, 1)
    return jnp.where(rows < HALF, upper, lower)


def pack_kernel(
    widths, tok_ref, emb_ref, in_ref, stud_ref, teach_ref, ft_ref, fs_ref, out_ref,
    emb_buf, data_buf, sems,
):
    vocab, channels = emb_ref.shape
    toks = tok_ref.shape[1]
    chunks = len(widths)
    dp = lax.axis_index("dp")
    teacher = dp < lax.axis_size("dp") // 2
    lead = lax.rem(dp, 2) == 0
    even = lax.rem(lax.axis_index("ctx"), 2) == 0

    def span(chunk):
        return pl.ds(sum(widths[:chunk]) // SUB * MESSAGE, widths[chunk] // SUB * MESSAGE)

    def copies(chunk, taps):
        cols = pl.ds(sum(widths[:chunk]), widths[chunk])
        sources = (
            (emb_ref.at[:, cols], emb_buf.at[:, cols]),
            (in_ref.at[0, :, cols], data_buf.at[0, :, cols]),
            (stud_ref.at[0, :, cols], data_buf.at[1, :, cols]),
            (teach_ref.at[0, :, cols], data_buf.at[2, :, cols]),
            (taps.at[:, cols], data_buf.at[3, :, cols]),
        )
        return [
            (src, dst, sems.at[chunk, n]) for n, (src, dst) in enumerate(sources)
        ]

    for chunk in range(chunks):
        for copy in copies(chunk, ft_ref)[:4]:
            pltpu.make_async_copy(*copy).start()

        @pl.when(teacher)
        def _():
            pltpu.make_async_copy(*copies(chunk, ft_ref)[4]).start()

        @pl.when(jnp.logical_not(teacher))
        def _():
            pltpu.make_async_copy(*copies(chunk, fs_ref)[4]).start()

    rows = lax.broadcasted_iota(jnp.int32, (vocab, toks), 0)
    one_hot = (rows == tok_ref[...]).astype(jnp.float32).T.astype(jnp.bfloat16)

    for chunk in range(chunks):
        for copy in copies(chunk, ft_ref):
            pltpu.make_async_copy(*copy).wait()
        pairs = widths[chunk] // (2 * SUB)
        cols = pl.ds(sum(widths[:chunk]), widths[chunk])
        values = dot(one_hot, emb_buf[:, cols])
        mixed = (data_buf[0, :, cols].astype(jnp.float32) * values).astype(jnp.bfloat16)
        parts = [
            turned(x).reshape(pairs, 2, SUB, toks)
            for x in (mixed, data_buf[1, :, cols], data_buf[2, :, cols], data_buf[3, :, cols])
        ]
        place = span(chunk)

        def store(tiles):
            out_ref[place, :] = (
                jnp.stack(tiles, axis=1).reshape(pairs * 2 * MESSAGE, toks).astype(jnp.bfloat16)
            )

        tap_upper = jnp.where(lead, parts[3][:, 0], half_turn(parts[3][:, 0]))
        tap_lower = jnp.where(lead, half_turn(parts[3][:, 1]), parts[3][:, 1])

        @pl.when(even)
        def _():
            mix, stud, teach = [half_turn(x[:, 1]) for x in parts[:3]]
            store([x[:, 0] for x in parts[:3]] + [
                halves(tap_upper, mix), halves(mix, stud), halves(stud, teach),
                halves(teach, tap_lower),
            ])

        @pl.when(jnp.logical_not(even))
        def _():
            mix, stud, teach = [x[:, 0] for x in parts[:3]]
            store([
                halves(tap_upper, mix), halves(mix, stud), halves(stud, teach),
                halves(teach, tap_lower),
            ] + [half_turn(x[:, 1]) for x in parts[:3]])


def pack(token_ids, embedding, in_gate, teacher_gate, student_gate, teacher_filter, student_filter):
    vocab, channels = embedding.shape
    toks = token_ids.shape[1]
    widths = (512,) * (channels // 512)
    here = pl.BlockSpec(memory_space=pl.ANY)
    return pl.pallas_call(
        functools.partial(pack_kernel, widths),
        in_specs=[pl.BlockSpec(memory_space=pltpu.VMEM)] + [here] * 6,
        out_specs=pl.BlockSpec(memory_space=pltpu.VMEM),
        out_shape=pltpu.VMEM((channels // SUB * MESSAGE, toks), jnp.bfloat16),
        scratch_shapes=[
            pltpu.VMEM((vocab, channels), jnp.bfloat16),
            pltpu.VMEM((4, toks, channels), jnp.bfloat16),
            pltpu.SemaphoreType.DMA((len(widths), 5)),
        ],
        compiler_params=pltpu.CompilerParams(vmem_limit_bytes=60 * MIB),
    )(token_ids, embedding, in_gate, student_gate, teacher_gate, teacher_filter, student_filter)


def filter_kernel(
    seqs, blocks, scale, in_ref, t1_ref, t1i_ref, turn_ref, t2_ref, t2i_ref, out_ref,
    x_ref, spec_ref, wave_ref, grad_ref, stud_ref, lag_ref,
):
    bf, f32 = jnp.bfloat16, jnp.float32
    toks = in_ref.shape[1]
    full = blocks * SUB
    half = full // 2
    pairs = blocks // 2
    cosines, sines = turn_ref[0], turn_ref[1]

    def received(seq):
        size = blocks * MESSAGE
        data = in_ref[pl.ds(seq * size, size), :].astype(f32)
        return data.reshape(pairs, 2 * MESSAGE // SUB, SUB, toks)

    def sets(data, part):
        even, odd = data[:, part], data[:, part + HALF]
        return jnp.concatenate(
            [halves(even, odd).reshape(half, toks), halves(odd, even).reshape(half, toks)], axis=0
        )

    def lanes(n):
        return pl.ds(n * toks, toks)

    def columns(x, n):
        return x[:, n * toks:(n + 1) * toks]

    for d in range(seqs):
        data = received(d)
        x_ref[:, lanes(d)] = sets(data, 0).astype(bf)
        rows = pl.ds((d % 2) * half, half)
        taps = half_turn(data[:, HALF - 1]) if d % 2 else data[:, HALF - 1]
        x_ref[rows, lanes(seqs + d // 2)] = taps.reshape(half, toks).astype(bf)

    def first(ref):
        return [dot(t1_ref[n], ref[pl.ds(n * half, half), :]) for n in range(2)]

    def second(outs, n):
        re = jnp.concatenate([columns(out[:half], n) for out in outs], axis=0)
        im = jnp.concatenate([columns(out[half:], n) for out in outs], axis=0)
        part = jnp.concatenate([re * cosines + im * sines, im * cosines - re * sines], axis=1)
        return dot(part.astype(bf), t2_ref[...])

    def back(prod):
        re, im = columns(prod, 0), columns(prod, 1)
        return re * cosines - im * sines, im * cosines + re * sines

    def keep(ref, n, re, im):
        ref[pl.ds(0, half), lanes(n)] = re[:half].astype(bf)
        ref[pl.ds(half, half), lanes(n)] = im[:half].astype(bf)
        ref[pl.ds(full, half), lanes(n)] = re[half:].astype(bf)
        ref[pl.ds(full + half, half), lanes(n)] = im[half:].astype(bf)

    def last(ref):
        return [dot(t1i_ref[n], ref[pl.ds(n * full, full), :]) for n in range(2)]

    outs = first(x_ref)
    taps = [second(outs, seqs + f) for f in range(2)]
    specs, waves = {}, {}
    for d in range(seqs + 2):
        if d < seqs:
            specs[d] = second(outs, d)
        if 0 <= d - 1 < seqs:
            spec = specs[d - 1]
            spec_ref[pl.ds((d - 1) * full, full), :] = spec
            ur, ui = columns(spec, 0), columns(spec, 1)
            for f in range(2):
                tr, ti = columns(taps[f], 0), columns(taps[f], 1)
                prod = jnp.concatenate([ur * tr - ui * ti, ur * ti + ui * tr], axis=1)
                waves[d - 1, f] = dot(prod.astype(bf), t2i_ref[...])
        if d >= 2:
            for f in range(2):
                keep(wave_ref, 2 * (d - 2) + f, *back(waves[d - 2, f]))

    for d in range(seqs):
        data = received(d)
        gate_s, gate_t = sets(data, 1), sets(data, 2)
        conv = jnp.concatenate(
            [dot(t1i_ref[n], wave_ref[pl.ds(n * full, full), pl.ds(2 * d * toks, 2 * toks)])
             for n in range(2)], axis=0,
        ).astype(bf).astype(f32)
        conv_t, conv_s = columns(conv, 0), columns(conv, 1)
        stud = gate_s * conv_s
        stud_ref[:, lanes(d)] = stud
        grad_ref[:, lanes(d)] = (gate_s * (stud - gate_t * conv_t)).astype(bf)

    outs = first(grad_ref)
    specs = [second(outs, d) for d in range(seqs)]
    sum_re = jnp.zeros((full, toks), f32)
    sum_im = jnp.zeros((full, toks), f32)
    for d in range(seqs):
        gr, gi = columns(specs[d], 0), columns(specs[d], 1)
        ur = spec_ref[pl.ds(d * full, full), lanes(0)]
        ui = spec_ref[pl.ds(d * full, full), lanes(1)]
        sum_re += gr * ur + gi * ui
        sum_im += gi * ur - gr * ui
    total = jnp.concatenate([sum_re, sum_im], axis=1)
    high = total.astype(bf)
    low = (total - high.astype(f32)).astype(bf)
    waves = dot(jnp.concatenate([high, low], axis=0), t2i_ref[...])
    re, im = back(waves[:full] + waves[full:])
    high_re, high_im = [x.astype(bf).astype(f32) for x in (re, im)]
    keep(lag_ref, 0, high_re, high_im)
    keep(lag_ref, 1, re - high_re, im - high_im)
    lags = [
        ((columns(x, 0) + columns(x, 1)) * scale).reshape(pairs, SUB, toks) for x in last(lag_ref)
    ]
    middle = (lags[0], half_turn(lags[1]))
    for d in range(seqs):
        first = stud_ref[pl.ds(0, half), lanes(d)].reshape(pairs, SUB, toks)
        second = stud_ref[pl.ds(half, half), lanes(d)].reshape(pairs, SUB, toks)
        tiles = jnp.stack([halves(first, second), middle[d % 2], halves(second, first)], axis=1)
        size = blocks * REPLY
        out_ref[pl.ds(d * size, size), :] = tiles.reshape(size, toks).astype(bf)


def filters(data, seqs, blocks):
    toks = data.shape[1]
    full = blocks * SUB
    scale = float(seqs * blocks * toks) ** -0.5
    bf, f32 = jnp.bfloat16, jnp.float32
    return pl.pallas_call(
        functools.partial(filter_kernel, seqs, blocks, scale),
        out_shape=jax.ShapeDtypeStruct((seqs * blocks * REPLY, toks), bf),
        scratch_shapes=[
            pltpu.VMEM((full, (seqs + 2) * toks), bf),
            pltpu.VMEM((seqs * full, 2 * toks), f32),
            pltpu.VMEM((2 * full, 2 * seqs * toks), bf),
            pltpu.VMEM((full, seqs * toks), bf),
            pltpu.VMEM((full, seqs * toks), f32),
            pltpu.VMEM((2 * full, 2 * toks), bf),
        ],
        compiler_params=pltpu.CompilerParams(vmem_limit_bytes=48 * MIB),
    )(data, *tables(blocks, toks))


def tiles(ref):
    rows, toks = ref.shape
    data = ref[...].astype(jnp.float32).reshape(rows // (3 * SUB), 3, SUB, toks)
    return data[:, 0], data[:, 1], data[:, 2]


def channels(upper, lower):
    pairs, _, toks = upper.shape
    both = jnp.stack([upper, lower], axis=1).reshape(pairs * 2 * SUB, toks)
    return both.astype(jnp.bfloat16).T


def student_kernel(in_ref, out_ref):
    even = lax.rem(lax.axis_index("ctx"), 2) == 0
    first, middle, last = tiles(in_ref)
    turned_last = half_turn(last)
    upper = jnp.where(even, first, halves(middle, first))
    lower = jnp.where(even, halves(half_turn(middle), turned_last), turned_last)
    out_ref[0] = channels(upper, lower)


def pick_kernel(in_ref, out_ref):
    even = lax.rem(lax.axis_index("ctx"), 2) == 0
    first, middle, last = tiles(in_ref)
    taps = jnp.where(even, halves(middle, last), halves(first, middle))
    out_ref[...] = taps.reshape(out_ref.shape).astype(jnp.bfloat16)


def lags_kernel(mine_ref, other_ref, out_ref):
    lead = lax.rem(lax.axis_index("dp"), 2) == 0
    rows, toks = mine_ref.shape
    mine, other = [
        ref[...].astype(jnp.float32).reshape(rows // SUB, SUB, toks)
        for ref in (mine_ref, other_ref)
    ]
    upper = jnp.where(lead, mine, other)
    lower = jnp.where(lead, other, mine)
    out_ref[...] = channels(
        halves(upper, half_turn(lower)), halves(half_turn(upper), lower)
    ).astype(jnp.float32)


def unpack(got, swap):
    rows, toks = got.shape
    count = rows // REPLY * SUB
    width = 1024
    message = pl.BlockSpec((width // SUB * REPLY, toks), lambda g: (g, 0))
    picked = pl.BlockSpec((width // 2, toks), lambda g: (g, 0))
    params = pltpu.CompilerParams(vmem_limit_bytes=32 * MIB)
    size = pl.CostEstimate(flops=MIB, bytes_accessed=2 * MIB, transcendentals=0)
    mine = pl.pallas_call(
        pick_kernel,
        out_shape=jax.ShapeDtypeStruct((count // 2, toks), jnp.bfloat16),
        compiler_params=params,
        cost_estimate=size,
    )(got)
    other = swap(mine)
    student = pl.pallas_call(
        student_kernel,
        grid=(count // width,),
        in_specs=[message],
        out_specs=pl.BlockSpec((1, toks, width), lambda g: (0, 0, g)),
        out_shape=jax.ShapeDtypeStruct((1, toks, count), jnp.bfloat16),
        compiler_params=params,
        cost_estimate=size,
    )(got)
    lags = pl.pallas_call(
        lags_kernel,
        grid=(count // width,),
        in_specs=[picked, picked],
        out_specs=pl.BlockSpec((toks, width), lambda g: (0, g)),
        out_shape=jax.ShapeDtypeStruct((toks, count), jnp.float32),
        compiler_params=params,
        cost_estimate=size,
    )(mine, other)
    return student, lags


def body(*args):
    seqs, blocks = lax.axis_size("dp"), lax.axis_size("ctx")

    def exchange(x):
        cut = x.reshape(seqs * blocks, -1, HALF, x.shape[1])
        got = lax.all_to_all(cut, ("dp", "ctx"), split_axis=0, concat_axis=0, tiled=True)
        return got.reshape(x.shape)

    got = exchange(filters(exchange(pack(*args)), seqs, blocks))
    partner = [(d, d + 1 - 2 * (d % 2)) for d in range(seqs)]
    return unpack(got, lambda x: lax.ppermute(x, "dp", partner))


def solution(mesh):
    placed = (
        P("dp", "ctx"),
        P(),
        P("dp", "ctx", None),
        P("dp", "ctx", None),
        P("dp", "ctx", None),
        P("ctx", None),
        P("ctx", None),
    )
    return jax.shard_map(
        body,
        mesh=mesh,
        in_specs=placed,
        out_specs=(P("dp", "ctx", None), P("ctx", None)),
        check_vma=False,
    )
```

```python
import functools

import jax
import jax.numpy as jnp
import numpy as np
from jax import lax
from jax.experimental import pallas as pl
from jax.experimental.pallas import tpu as pltpu
from jax.sharding import PartitionSpec as P

SUB = 8
HALF = 4
MESSAGE = 28
REPLY = 12
MIB = 1 << 20


def tables(blocks, inner):
    span = 2 * blocks * inner
    freq = np.arange(blocks, dtype=np.float64) + 0.5
    pos = np.arange(blocks, dtype=np.float64)
    lane = np.arange(inner, dtype=np.float64)
    angle = 2.0 * np.pi * ((freq[:, None] * pos[None, :]) % (2 * blocks)) / (2 * blocks)
    both = np.stack([np.cos(angle), -np.sin(angle)])
    spread = np.einsum("rka,im->rkiam", both, np.eye(HALF))
    swapped = spread.reshape(2, blocks, HALF, blocks // 2, 2, HALF)[:, :, :, :, ::-1]
    shape = (2 * blocks * HALF, blocks * HALF)
    first = np.stack([spread.reshape(shape), swapped.reshape(shape)])
    turn = 2.0 * np.pi * (freq[:, None] * lane[None, :]) / span
    turn = np.repeat(np.stack([np.cos(turn), np.sin(turn)]), HALF, axis=1)
    turn = np.concatenate([turn, turn], axis=1)
    angle = 2.0 * np.pi * ((lane[:, None] * lane[None, :]) % inner) / inner
    cosines, sines = np.cos(angle), np.sin(angle)
    second = np.block([[cosines, -sines], [sines, cosines]])
    bf = jnp.bfloat16
    return (
        jnp.asarray(first, bf),
        jnp.asarray(first.transpose(0, 2, 1) * (2.0 / span), bf),
        jnp.asarray(turn, jnp.float32),
        jnp.asarray(second, bf),
        jnp.asarray(second.T, bf),
    )


def dot(a, b):
    return jnp.dot(a, b, preferred_element_type=jnp.float32)


def turned(x):
    return x.T.astype(jnp.float32)


def half_turn(x):
    return jnp.concatenate([x[:, HALF:], x[:, :HALF]], axis=1)


def halves(upper, lower):
    rows = lax.broadcasted_iota(jnp.int32, upper.shape, 1)
    return jnp.where(rows < HALF, upper, lower)


def pack_kernel(
    widths, tok_ref, emb_ref, in_ref, stud_ref, teach_ref, ft_ref, fs_ref, out_ref,
    emb_buf, data_buf, sems,
):
    vocab, channels = emb_ref.shape
    toks = tok_ref.shape[1]
    chunks = len(widths)
    dp = lax.axis_index("dp")
    teacher = dp < lax.axis_size("dp") // 2
    lead = lax.rem(dp, 2) == 0
    even = lax.rem(lax.axis_index("ctx"), 2) == 0

    def span(chunk):
        return pl.ds(sum(widths[:chunk]) // SUB * MESSAGE, widths[chunk] // SUB * MESSAGE)

    def copies(chunk, taps):
        cols = pl.ds(sum(widths[:chunk]), widths[chunk])
        sources = (
            (emb_ref.at[:, cols], emb_buf.at[:, cols]),
            (in_ref.at[0, :, cols], data_buf.at[0, :, cols]),
            (stud_ref.at[0, :, cols], data_buf.at[1, :, cols]),
            (teach_ref.at[0, :, cols], data_buf.at[2, :, cols]),
            (taps.at[:, cols], data_buf.at[3, :, cols]),
        )
        return [
            (src, dst, sems.at[chunk, n]) for n, (src, dst) in enumerate(sources)
        ]

    for chunk in range(chunks):
        for copy in copies(chunk, ft_ref)[:4]:
            pltpu.make_async_copy(*copy).start()

        @pl.when(teacher)
        def _():
            pltpu.make_async_copy(*copies(chunk, ft_ref)[4]).start()

        @pl.when(jnp.logical_not(teacher))
        def _():
            pltpu.make_async_copy(*copies(chunk, fs_ref)[4]).start()

    rows = lax.broadcasted_iota(jnp.int32, (vocab, toks), 0)
    one_hot = (rows == tok_ref[...]).astype(jnp.float32).T.astype(jnp.bfloat16)

    for chunk in range(chunks):
        for copy in copies(chunk, ft_ref):
            pltpu.make_async_copy(*copy).wait()
        pairs = widths[chunk] // (2 * SUB)
        cols = pl.ds(sum(widths[:chunk]), widths[chunk])
        values = dot(one_hot, emb_buf[:, cols])
        mixed = (data_buf[0, :, cols].astype(jnp.float32) * values).astype(jnp.bfloat16)
        parts = [
            turned(x).reshape(pairs, 2, SUB, toks)
            for x in (mixed, data_buf[1, :, cols], data_buf[2, :, cols], data_buf[3, :, cols])
        ]
        place = span(chunk)

        def store(tiles):
            out_ref[place, :] = (
                jnp.stack(tiles, axis=1).reshape(pairs * 2 * MESSAGE, toks).astype(jnp.bfloat16)
            )

        tap_upper = jnp.where(lead, parts[3][:, 0], half_turn(parts[3][:, 0]))
        tap_lower = jnp.where(lead, half_turn(parts[3][:, 1]), parts[3][:, 1])

        @pl.when(even)
        def _():
            mix, stud, teach = [half_turn(x[:, 1]) for x in parts[:3]]
            store([x[:, 0] for x in parts[:3]] + [
                halves(tap_upper, mix), halves(mix, stud), halves(stud, teach),
                halves(teach, tap_lower),
            ])

        @pl.when(jnp.logical_not(even))
        def _():
            mix, stud, teach = [x[:, 0] for x in parts[:3]]
            store([
                halves(tap_upper, mix), halves(mix, stud), halves(stud, teach),
                halves(teach, tap_lower),
            ] + [half_turn(x[:, 1]) for x in parts[:3]])


def pack(token_ids, embedding, in_gate, teacher_gate, student_gate, teacher_filter, student_filter):
    vocab, channels = embedding.shape
    toks = token_ids.shape[1]
    widths = (512,) * (channels // 512)
    here = pl.BlockSpec(memory_space=pl.ANY)
    return pl.pallas_call(
        functools.partial(pack_kernel, widths),
        in_specs=[pl.BlockSpec(memory_space=pltpu.VMEM)] + [here] * 6,
        out_specs=pl.BlockSpec(memory_space=pltpu.VMEM),
        out_shape=pltpu.VMEM((channels // SUB * MESSAGE, toks), jnp.bfloat16),
        scratch_shapes=[
            pltpu.VMEM((vocab, channels), jnp.bfloat16),
            pltpu.VMEM((4, toks, channels), jnp.bfloat16),
            pltpu.SemaphoreType.DMA((len(widths), 5)),
        ],
        compiler_params=pltpu.CompilerParams(vmem_limit_bytes=60 * MIB),
    )(token_ids, embedding, in_gate, student_gate, teacher_gate, teacher_filter, student_filter)


def filter_kernel(
    seqs, blocks, scale, in_ref, t1_ref, t1i_ref, turn_ref, t2_ref, t2i_ref, out_ref,
    x_ref, spec_ref, wave_ref, grad_ref, stud_ref, lag_ref,
):
    bf, f32 = jnp.bfloat16, jnp.float32
    toks = in_ref.shape[1]
    full = blocks * SUB
    half = full // 2
    pairs = blocks // 2
    cosines, sines = turn_ref[0], turn_ref[1]

    def received(seq):
        size = blocks * MESSAGE
        data = in_ref[pl.ds(seq * size, size), :].astype(f32)
        return data.reshape(pairs, 2 * MESSAGE // SUB, SUB, toks)

    def sets(data, part):
        even, odd = data[:, part], data[:, part + HALF]
        return jnp.concatenate(
            [halves(even, odd).reshape(half, toks), halves(odd, even).reshape(half, toks)], axis=0
        )

    def lanes(n):
        return pl.ds(n * toks, toks)

    def columns(x, n):
        return x[:, n * toks:(n + 1) * toks]

    for d in range(seqs):
        data = received(d)
        x_ref[:, lanes(d)] = sets(data, 0).astype(bf)
        rows = pl.ds((d % 2) * half, half)
        taps = half_turn(data[:, HALF - 1]) if d % 2 else data[:, HALF - 1]
        x_ref[rows, lanes(seqs + d // 2)] = taps.reshape(half, toks).astype(bf)

    def first(ref):
        return [dot(t1_ref[n], ref[pl.ds(n * half, half), :]) for n in range(2)]

    def second(outs, n):
        re = jnp.concatenate([columns(out[:half], n) for out in outs], axis=0)
        im = jnp.concatenate([columns(out[half:], n) for out in outs], axis=0)
        part = jnp.concatenate([re * cosines + im * sines, im * cosines - re * sines], axis=1)
        return dot(part.astype(bf), t2_ref[...])

    def back(prod):
        re, im = columns(prod, 0), columns(prod, 1)
        return re * cosines - im * sines, im * cosines + re * sines

    def keep(ref, n, re, im):
        ref[pl.ds(0, half), lanes(n)] = re[:half].astype(bf)
        ref[pl.ds(half, half), lanes(n)] = im[:half].astype(bf)
        ref[pl.ds(full, half), lanes(n)] = re[half:].astype(bf)
        ref[pl.ds(full + half, half), lanes(n)] = im[half:].astype(bf)

    def last(ref):
        return [dot(t1i_ref[n], ref[pl.ds(n * full, full), :]) for n in range(2)]

    outs = first(x_ref)
    taps = [second(outs, seqs + f) for f in range(2)]
    specs, waves = {}, {}
    for d in range(seqs + 2):
        if d < seqs:
            specs[d] = second(outs, d)
        if 0 <= d - 1 < seqs:
            spec = specs[d - 1]
            spec_ref[pl.ds((d - 1) * full, full), :] = spec
            ur, ui = columns(spec, 0), columns(spec, 1)
            for f in range(2):
                tr, ti = columns(taps[f], 0), columns(taps[f], 1)
                prod = jnp.concatenate([ur * tr - ui * ti, ur * ti + ui * tr], axis=1)
                waves[d - 1, f] = dot(prod.astype(bf), t2i_ref[...])
        if d >= 2:
            for f in range(2):
                keep(wave_ref, 2 * (d - 2) + f, *back(waves[d - 2, f]))

    for d in range(seqs):
        data = received(d)
        gate_s, gate_t = sets(data, 1), sets(data, 2)
        conv = jnp.concatenate(
            [dot(t1i_ref[n], wave_ref[pl.ds(n * full, full), pl.ds(2 * d * toks, 2 * toks)])
             for n in range(2)], axis=0,
        ).astype(bf).astype(f32)
        conv_t, conv_s = columns(conv, 0), columns(conv, 1)
        stud = gate_s * conv_s
        stud_ref[:, lanes(d)] = stud
        grad_ref[:, lanes(d)] = (gate_s * (stud - gate_t * conv_t)).astype(bf)

    outs = first(grad_ref)
    specs = [second(outs, d) for d in range(seqs)]
    sum_re = jnp.zeros((full, toks), f32)
    sum_im = jnp.zeros((full, toks), f32)
    for d in range(seqs):
        gr, gi = columns(specs[d], 0), columns(specs[d], 1)
        ur = spec_ref[pl.ds(d * full, full), lanes(0)]
        ui = spec_ref[pl.ds(d * full, full), lanes(1)]
        sum_re += gr * ur + gi * ui
        sum_im += gi * ur - gr * ui
    total = jnp.concatenate([sum_re, sum_im], axis=1)
    high = total.astype(bf)
    low = (total - high.astype(f32)).astype(bf)
    waves = dot(jnp.concatenate([high, low], axis=0), t2i_ref[...])
    re, im = back(waves[:full] + waves[full:])
    high_re, high_im = [x.astype(bf).astype(f32) for x in (re, im)]
    keep(lag_ref, 0, high_re, high_im)
    keep(lag_ref, 1, re - high_re, im - high_im)
    lags = [
        ((columns(x, 0) + columns(x, 1)) * scale).reshape(pairs, SUB, toks) for x in last(lag_ref)
    ]
    middle = (lags[0], half_turn(lags[1]))
    for d in range(seqs):
        first = stud_ref[pl.ds(0, half), lanes(d)].reshape(pairs, SUB, toks)
        second = stud_ref[pl.ds(half, half), lanes(d)].reshape(pairs, SUB, toks)
        tiles = jnp.stack([halves(first, second), middle[d % 2], halves(second, first)], axis=1)
        size = blocks * REPLY
        out_ref[pl.ds(d * size, size), :] = tiles.reshape(size, toks).astype(bf)


def filters(data, seqs, blocks):
    toks = data.shape[1]
    full = blocks * SUB
    scale = float(seqs * blocks * toks) ** -0.5
    bf, f32 = jnp.bfloat16, jnp.float32
    return pl.pallas_call(
        functools.partial(filter_kernel, seqs, blocks, scale),
        out_shape=jax.ShapeDtypeStruct((seqs * blocks * REPLY, toks), bf),
        scratch_shapes=[
            pltpu.VMEM((full, (seqs + 2) * toks), bf),
            pltpu.VMEM((seqs * full, 2 * toks), f32),
            pltpu.VMEM((2 * full, 2 * seqs * toks), bf),
            pltpu.VMEM((full, seqs * toks), bf),
            pltpu.VMEM((full, seqs * toks), f32),
            pltpu.VMEM((2 * full, 2 * toks), bf),
        ],
        compiler_params=pltpu.CompilerParams(vmem_limit_bytes=48 * MIB),
    )(data, *tables(blocks, toks))


def tiles(ref):
    rows, toks = ref.shape
    data = ref[...].astype(jnp.float32).reshape(rows // (3 * SUB), 3, SUB, toks)
    return data[:, 0], data[:, 1], data[:, 2]


def channels(upper, lower):
    pairs, _, toks = upper.shape
    both = jnp.stack([upper, lower], axis=1).reshape(pairs * 2 * SUB, toks)
    return both.astype(jnp.bfloat16).T


def leave(out_ref, buf, sems, parts, count):
    width = buf.shape[1] // parts
    copies = []
    for n in range(parts):
        cols = pl.ds(n * width, width)
        buf[:, cols] = count(n)
        copies.append(pltpu.make_async_copy(buf.at[:, cols], out_ref.at[:, cols], sems.at[n]))
        copies[-1].start()
    for copy in copies:
        copy.wait()


def cut(x, n, parts):
    size = x.shape[0] // parts
    return x[n * size:(n + 1) * size]


def student_kernel(parts, in_ref, out_ref, buf, sems):
    even = lax.rem(lax.axis_index("ctx"), 2) == 0
    rows = in_ref.shape[0] // parts

    def count(n):
        first, middle, last = tiles(in_ref.at[pl.ds(n * rows, rows), :])
        turned_last = half_turn(last)
        upper = jnp.where(even, first, halves(middle, first))
        lower = jnp.where(even, halves(half_turn(middle), turned_last), turned_last)
        return channels(upper, lower)

    leave(out_ref.at[0], buf, sems, parts, count)


def pick_kernel(in_ref, out_ref):
    even = lax.rem(lax.axis_index("ctx"), 2) == 0
    first, middle, last = tiles(in_ref)
    taps = jnp.where(even, halves(middle, last), halves(first, middle))
    out_ref[...] = taps.reshape(out_ref.shape).astype(jnp.bfloat16)


def lags_kernel(parts, mine_ref, other_ref, out_ref, buf, sems):
    lead = lax.rem(lax.axis_index("dp"), 2) == 0
    rows, toks = mine_ref.shape
    rows //= parts

    def count(n):
        mine, other = [
            ref[pl.ds(n * rows, rows), :].astype(jnp.float32).reshape(rows // SUB, SUB, toks)
            for ref in (mine_ref, other_ref)
        ]
        upper = jnp.where(lead, mine, other)
        lower = jnp.where(lead, other, mine)
        return channels(
            halves(upper, half_turn(lower)), halves(half_turn(upper), lower)
        ).astype(jnp.float32)

    leave(out_ref, buf, sems, parts, count)


def unpack(got, swap):
    rows, toks = got.shape
    count = rows // REPLY * SUB
    parts = 4
    params = pltpu.CompilerParams(vmem_limit_bytes=32 * MIB)
    size = pl.CostEstimate(flops=MIB, bytes_accessed=2 * MIB, transcendentals=0)
    mine = pl.pallas_call(
        pick_kernel,
        out_shape=jax.ShapeDtypeStruct((count // 2, toks), jnp.bfloat16),
        compiler_params=params,
        cost_estimate=size,
    )(got)
    other = swap(mine)
    student = pl.pallas_call(
        functools.partial(student_kernel, parts),
        in_specs=[pl.BlockSpec(memory_space=pltpu.VMEM)],
        out_specs=pl.BlockSpec(memory_space=pl.ANY),
        scratch_shapes=[
            pltpu.VMEM((toks, count), jnp.bfloat16), pltpu.SemaphoreType.DMA((parts,)),
        ],
        out_shape=jax.ShapeDtypeStruct((1, toks, count), jnp.bfloat16),
        compiler_params=params,
        cost_estimate=size,
    )(got)
    lags = pl.pallas_call(
        functools.partial(lags_kernel, parts),
        in_specs=[pl.BlockSpec(memory_space=pltpu.VMEM)] * 2,
        out_specs=pl.BlockSpec(memory_space=pl.ANY),
        scratch_shapes=[
            pltpu.VMEM((toks, count), jnp.float32), pltpu.SemaphoreType.DMA((parts,)),
        ],
        out_shape=jax.ShapeDtypeStruct((toks, count), jnp.float32),
        compiler_params=params,
        cost_estimate=size,
    )(mine, other)
    return student, lags


def body(*args):
    seqs, blocks = lax.axis_size("dp"), lax.axis_size("ctx")

    def exchange(x):
        cut = x.reshape(seqs * blocks, -1, HALF, x.shape[1])
        got = lax.all_to_all(cut, ("dp", "ctx"), split_axis=0, concat_axis=0, tiled=True)
        return got.reshape(x.shape)

    got = exchange(filters(exchange(pack(*args)), seqs, blocks))
    partner = [(d, d + 1 - 2 * (d % 2)) for d in range(seqs)]
    return unpack(got, lambda x: lax.ppermute(x, "dp", partner))


def solution(mesh):
    placed = (
        P("dp", "ctx"),
        P(),
        P("dp", "ctx", None),
        P("dp", "ctx", None),
        P("dp", "ctx", None),
        P("ctx", None),
        P("ctx", None),
    )
    return jax.shard_map(
        body,
        mesh=mesh,
        in_specs=placed,
        out_specs=(P("dp", "ctx", None), P("ctx", None)),
        check_vma=False,
    )
```

```python
import functools

import jax
import jax.numpy as jnp
import numpy as np
from jax import lax
from jax.experimental import pallas as pl
from jax.experimental.pallas import tpu as pltpu
from jax.sharding import PartitionSpec as P

SUB = 8
HALF = 4
MESSAGE = 28
REPLY = 12
MIB = 1 << 20


def tables(blocks, inner):
    span = 2 * blocks * inner
    freq = np.arange(blocks, dtype=np.float64) + 0.5
    pos = np.arange(blocks, dtype=np.float64)
    lane = np.arange(inner, dtype=np.float64)
    angle = 2.0 * np.pi * ((freq[:, None] * pos[None, :]) % (2 * blocks)) / (2 * blocks)
    both = np.stack([np.cos(angle), -np.sin(angle)])
    spread = np.einsum("rka,im->rkiam", both, np.eye(HALF))
    swapped = spread.reshape(2, blocks, HALF, blocks // 2, 2, HALF)[:, :, :, :, ::-1]
    shape = (2 * blocks * HALF, blocks * HALF)
    first = np.stack([spread.reshape(shape), swapped.reshape(shape)])
    turn = 2.0 * np.pi * (freq[:, None] * lane[None, :]) / span
    turn = np.repeat(np.stack([np.cos(turn), np.sin(turn)]), HALF, axis=1)
    turn = np.concatenate([turn, turn], axis=1)
    angle = 2.0 * np.pi * ((lane[:, None] * lane[None, :]) % inner) / inner
    cosines, sines = np.cos(angle), np.sin(angle)
    second = np.block([[cosines, -sines], [sines, cosines]])
    bf = jnp.bfloat16
    return (
        jnp.asarray(first, bf),
        jnp.asarray(first.transpose(0, 2, 1) * (2.0 / span), bf),
        jnp.asarray(turn, jnp.float32),
        jnp.asarray(second, bf),
        jnp.asarray(second.T, bf),
    )


def dot(a, b):
    return jnp.dot(a, b, preferred_element_type=jnp.float32)


def turned(x):
    return x.T.astype(jnp.float32)


def half_turn(x):
    return jnp.concatenate([x[:, HALF:], x[:, :HALF]], axis=1)


def halves(upper, lower):
    rows = lax.broadcasted_iota(jnp.int32, upper.shape, 1)
    return jnp.where(rows < HALF, upper, lower)


def pack_kernel(
    widths, tok_ref, emb_ref, in_ref, stud_ref, teach_ref, ft_ref, fs_ref, out_ref,
    emb_buf, data_buf, sems,
):
    vocab, channels = emb_ref.shape
    toks = tok_ref.shape[1]
    chunks = len(widths)
    dp = lax.axis_index("dp")
    teacher = dp < lax.axis_size("dp") // 2
    lead = lax.rem(dp, 2) == 0
    even = lax.rem(lax.axis_index("ctx"), 2) == 0

    def span(chunk):
        return pl.ds(sum(widths[:chunk]) // SUB * MESSAGE, widths[chunk] // SUB * MESSAGE)

    def copies(chunk, taps):
        cols = pl.ds(sum(widths[:chunk]), widths[chunk])
        sources = (
            (emb_ref.at[:, cols], emb_buf.at[:, cols]),
            (in_ref.at[0, :, cols], data_buf.at[0, :, cols]),
            (stud_ref.at[0, :, cols], data_buf.at[1, :, cols]),
            (teach_ref.at[0, :, cols], data_buf.at[2, :, cols]),
            (taps.at[:, cols], data_buf.at[3, :, cols]),
        )
        return [
            (src, dst, sems.at[chunk, n]) for n, (src, dst) in enumerate(sources)
        ]

    for chunk in range(chunks):
        for copy in copies(chunk, ft_ref)[:4]:
            pltpu.make_async_copy(*copy).start()

        @pl.when(teacher)
        def _():
            pltpu.make_async_copy(*copies(chunk, ft_ref)[4]).start()

        @pl.when(jnp.logical_not(teacher))
        def _():
            pltpu.make_async_copy(*copies(chunk, fs_ref)[4]).start()

    rows = lax.broadcasted_iota(jnp.int32, (vocab, toks), 0)
    one_hot = (rows == tok_ref[...]).astype(jnp.float32).T.astype(jnp.bfloat16)

    for chunk in range(chunks):
        for copy in copies(chunk, ft_ref):
            pltpu.make_async_copy(*copy).wait()
        pairs = widths[chunk] // (2 * SUB)
        cols = pl.ds(sum(widths[:chunk]), widths[chunk])
        values = dot(one_hot, emb_buf[:, cols])
        mixed = (data_buf[0, :, cols].astype(jnp.float32) * values).astype(jnp.bfloat16)
        parts = [
            turned(x).reshape(pairs, 2, SUB, toks)
            for x in (mixed, data_buf[1, :, cols], data_buf[2, :, cols], data_buf[3, :, cols])
        ]
        place = span(chunk)

        def store(tiles):
            out_ref[place, :] = (
                jnp.stack(tiles, axis=1).reshape(pairs * 2 * MESSAGE, toks).astype(jnp.bfloat16)
            )

        tap_upper = jnp.where(lead, parts[3][:, 0], half_turn(parts[3][:, 0]))
        tap_lower = jnp.where(lead, half_turn(parts[3][:, 1]), parts[3][:, 1])

        @pl.when(even)
        def _():
            mix, stud, teach = [half_turn(x[:, 1]) for x in parts[:3]]
            store([x[:, 0] for x in parts[:3]] + [
                halves(tap_upper, mix), halves(mix, stud), halves(stud, teach),
                halves(teach, tap_lower),
            ])

        @pl.when(jnp.logical_not(even))
        def _():
            mix, stud, teach = [x[:, 0] for x in parts[:3]]
            store([
                halves(tap_upper, mix), halves(mix, stud), halves(stud, teach),
                halves(teach, tap_lower),
            ] + [half_turn(x[:, 1]) for x in parts[:3]])


def pack(token_ids, embedding, in_gate, teacher_gate, student_gate, teacher_filter, student_filter):
    vocab, channels = embedding.shape
    toks = token_ids.shape[1]
    widths = (channels * 5 // 8, channels * 3 // 8)
    here = pl.BlockSpec(memory_space=pl.ANY)
    return pl.pallas_call(
        functools.partial(pack_kernel, widths),
        in_specs=[pl.BlockSpec(memory_space=pltpu.VMEM)] + [here] * 6,
        out_specs=pl.BlockSpec(memory_space=pltpu.VMEM),
        out_shape=pltpu.VMEM((channels // SUB * MESSAGE, toks), jnp.bfloat16),
        scratch_shapes=[
            pltpu.VMEM((vocab, channels), jnp.bfloat16),
            pltpu.VMEM((4, toks, channels), jnp.bfloat16),
            pltpu.SemaphoreType.DMA((len(widths), 5)),
        ],
        compiler_params=pltpu.CompilerParams(vmem_limit_bytes=60 * MIB),
    )(token_ids, embedding, in_gate, student_gate, teacher_gate, teacher_filter, student_filter)


def filter_kernel(
    seqs, blocks, scale, in_ref, t1_ref, t1i_ref, turn_ref, t2_ref, t2i_ref, out_ref,
    x_ref, spec_ref, wave_ref, grad_ref, stud_ref, lag_ref,
):
    bf, f32 = jnp.bfloat16, jnp.float32
    toks = in_ref.shape[1]
    full = blocks * SUB
    half = full // 2
    pairs = blocks // 2
    cosines, sines = turn_ref[0], turn_ref[1]

    def received(seq):
        size = blocks * MESSAGE
        data = in_ref[pl.ds(seq * size, size), :].astype(f32)
        return data.reshape(pairs, 2 * MESSAGE // SUB, SUB, toks)

    def sets(data, part):
        even, odd = data[:, part], data[:, part + HALF]
        return jnp.concatenate(
            [halves(even, odd).reshape(half, toks), halves(odd, even).reshape(half, toks)], axis=0
        )

    def lanes(n):
        return pl.ds(n * toks, toks)

    def columns(x, n):
        return x[:, n * toks:(n + 1) * toks]

    for d in range(seqs):
        data = received(d)
        x_ref[:, lanes(d)] = sets(data, 0).astype(bf)
        rows = pl.ds((d % 2) * half, half)
        taps = half_turn(data[:, HALF - 1]) if d % 2 else data[:, HALF - 1]
        x_ref[rows, lanes(seqs + d // 2)] = taps.reshape(half, toks).astype(bf)

    def first(ref):
        return [dot(t1_ref[n], ref[pl.ds(n * half, half), :]) for n in range(2)]

    def second(outs, n):
        re = jnp.concatenate([columns(out[:half], n) for out in outs], axis=0)
        im = jnp.concatenate([columns(out[half:], n) for out in outs], axis=0)
        part = jnp.concatenate([re * cosines + im * sines, im * cosines - re * sines], axis=1)
        return dot(part.astype(bf), t2_ref[...])

    def back(prod):
        re, im = columns(prod, 0), columns(prod, 1)
        return re * cosines - im * sines, im * cosines + re * sines

    def keep(ref, n, re, im):
        ref[pl.ds(0, half), lanes(n)] = re[:half].astype(bf)
        ref[pl.ds(half, half), lanes(n)] = im[:half].astype(bf)
        ref[pl.ds(full, half), lanes(n)] = re[half:].astype(bf)
        ref[pl.ds(full + half, half), lanes(n)] = im[half:].astype(bf)

    def last(ref):
        return [dot(t1i_ref[n], ref[pl.ds(n * full, full), :]) for n in range(2)]

    outs = first(x_ref)
    taps = [second(outs, seqs + f) for f in range(2)]
    specs, waves = {}, {}
    for d in range(seqs + 2):
        if d < seqs:
            specs[d] = second(outs, d)
        if 0 <= d - 1 < seqs:
            spec = specs[d - 1]
            spec_ref[pl.ds((d - 1) * full, full), :] = spec
            ur, ui = columns(spec, 0), columns(spec, 1)
            for f in range(2):
                tr, ti = columns(taps[f], 0), columns(taps[f], 1)
                prod = jnp.concatenate([ur * tr - ui * ti, ur * ti + ui * tr], axis=1)
                waves[d - 1, f] = dot(prod.astype(bf), t2i_ref[...])
        if d >= 2:
            for f in range(2):
                keep(wave_ref, 2 * (d - 2) + f, *back(waves[d - 2, f]))

    for d in range(seqs):
        data = received(d)
        gate_s, gate_t = sets(data, 1), sets(data, 2)
        conv = jnp.concatenate(
            [dot(t1i_ref[n], wave_ref[pl.ds(n * full, full), pl.ds(2 * d * toks, 2 * toks)])
             for n in range(2)], axis=0,
        ).astype(bf).astype(f32)
        conv_t, conv_s = columns(conv, 0), columns(conv, 1)
        stud = gate_s * conv_s
        stud_ref[:, lanes(d)] = stud
        grad_ref[:, lanes(d)] = (gate_s * (stud - gate_t * conv_t)).astype(bf)

    outs = first(grad_ref)
    specs = [second(outs, d) for d in range(seqs)]
    sum_re = jnp.zeros((full, toks), f32)
    sum_im = jnp.zeros((full, toks), f32)
    for d in range(seqs):
        gr, gi = columns(specs[d], 0), columns(specs[d], 1)
        ur = spec_ref[pl.ds(d * full, full), lanes(0)]
        ui = spec_ref[pl.ds(d * full, full), lanes(1)]
        sum_re += gr * ur + gi * ui
        sum_im += gi * ur - gr * ui
    total = jnp.concatenate([sum_re, sum_im], axis=1)
    high = total.astype(bf)
    low = (total - high.astype(f32)).astype(bf)
    waves = dot(jnp.concatenate([high, low], axis=0), t2i_ref[...])
    re, im = back(waves[:full] + waves[full:])
    high_re, high_im = [x.astype(bf).astype(f32) for x in (re, im)]
    keep(lag_ref, 0, high_re, high_im)
    keep(lag_ref, 1, re - high_re, im - high_im)
    lags = [
        ((columns(x, 0) + columns(x, 1)) * scale).reshape(pairs, SUB, toks) for x in last(lag_ref)
    ]
    middle = (lags[0], half_turn(lags[1]))
    for d in range(seqs):
        first = stud_ref[pl.ds(0, half), lanes(d)].reshape(pairs, SUB, toks)
        second = stud_ref[pl.ds(half, half), lanes(d)].reshape(pairs, SUB, toks)
        tiles = jnp.stack([halves(first, second), middle[d % 2], halves(second, first)], axis=1)
        size = blocks * REPLY
        out_ref[pl.ds(d * size, size), :] = tiles.reshape(size, toks).astype(bf)


def filters(data, seqs, blocks):
    toks = data.shape[1]
    full = blocks * SUB
    scale = float(seqs * blocks * toks) ** -0.5
    bf, f32 = jnp.bfloat16, jnp.float32
    return pl.pallas_call(
        functools.partial(filter_kernel, seqs, blocks, scale),
        out_shape=jax.ShapeDtypeStruct((seqs * blocks * REPLY, toks), bf),
        scratch_shapes=[
            pltpu.VMEM((full, (seqs + 2) * toks), bf),
            pltpu.VMEM((seqs * full, 2 * toks), f32),
            pltpu.VMEM((2 * full, 2 * seqs * toks), bf),
            pltpu.VMEM((full, seqs * toks), bf),
            pltpu.VMEM((full, seqs * toks), f32),
            pltpu.VMEM((2 * full, 2 * toks), bf),
        ],
        compiler_params=pltpu.CompilerParams(vmem_limit_bytes=48 * MIB),
    )(data, *tables(blocks, toks))


def tiles(ref):
    rows, toks = ref.shape
    data = ref[...].astype(jnp.float32).reshape(rows // (3 * SUB), 3, SUB, toks)
    return data[:, 0], data[:, 1], data[:, 2]


def channels(upper, lower):
    pairs, _, toks = upper.shape
    both = jnp.stack([upper, lower], axis=1).reshape(pairs * 2 * SUB, toks)
    return both.astype(jnp.bfloat16).T


def leave(out_ref, buf, sems, parts, count):
    width = buf.shape[1] // parts
    copies = []
    for n in range(parts):
        cols = pl.ds(n * width, width)
        buf[:, cols] = count(n)
        copies.append(pltpu.make_async_copy(buf.at[:, cols], out_ref.at[:, cols], sems.at[n]))
        copies[-1].start()
    for copy in copies:
        copy.wait()


def cut(x, n, parts):
    size = x.shape[0] // parts
    return x[n * size:(n + 1) * size]


def student_kernel(parts, in_ref, out_ref, buf, sems):
    even = lax.rem(lax.axis_index("ctx"), 2) == 0
    rows = in_ref.shape[0] // parts

    def count(n):
        first, middle, last = tiles(in_ref.at[pl.ds(n * rows, rows), :])
        turned_last = half_turn(last)
        upper = jnp.where(even, first, halves(middle, first))
        lower = jnp.where(even, halves(half_turn(middle), turned_last), turned_last)
        return channels(upper, lower)

    leave(out_ref.at[0], buf, sems, parts, count)


def pick_kernel(in_ref, out_ref):
    even = lax.rem(lax.axis_index("ctx"), 2) == 0
    first, middle, last = tiles(in_ref)
    taps = jnp.where(even, halves(middle, last), halves(first, middle))
    out_ref[...] = taps.reshape(out_ref.shape).astype(jnp.bfloat16)


def lags_kernel(parts, mine_ref, other_ref, out_ref, buf, sems):
    lead = lax.rem(lax.axis_index("dp"), 2) == 0
    rows, toks = mine_ref.shape
    rows //= parts

    def count(n):
        mine, other = [
            ref[pl.ds(n * rows, rows), :].astype(jnp.float32).reshape(rows // SUB, SUB, toks)
            for ref in (mine_ref, other_ref)
        ]
        upper = jnp.where(lead, mine, other)
        lower = jnp.where(lead, other, mine)
        return channels(
            halves(upper, half_turn(lower)), halves(half_turn(upper), lower)
        ).astype(jnp.float32)

    leave(out_ref, buf, sems, parts, count)


def unpack(got, swap):
    rows, toks = got.shape
    count = rows // REPLY * SUB
    parts = 4
    params = pltpu.CompilerParams(vmem_limit_bytes=32 * MIB)
    size = pl.CostEstimate(flops=MIB, bytes_accessed=2 * MIB, transcendentals=0)
    mine = pl.pallas_call(
        pick_kernel,
        out_shape=jax.ShapeDtypeStruct((count // 2, toks), jnp.bfloat16),
        compiler_params=params,
        cost_estimate=size,
    )(got)
    other = swap(mine)
    student = pl.pallas_call(
        functools.partial(student_kernel, parts),
        in_specs=[pl.BlockSpec(memory_space=pltpu.VMEM)],
        out_specs=pl.BlockSpec(memory_space=pl.ANY),
        scratch_shapes=[
            pltpu.VMEM((toks, count), jnp.bfloat16), pltpu.SemaphoreType.DMA((parts,)),
        ],
        out_shape=jax.ShapeDtypeStruct((1, toks, count), jnp.bfloat16),
        compiler_params=params,
        cost_estimate=size,
    )(got)
    lags = pl.pallas_call(
        functools.partial(lags_kernel, parts),
        in_specs=[pl.BlockSpec(memory_space=pltpu.VMEM)] * 2,
        out_specs=pl.BlockSpec(memory_space=pl.ANY),
        scratch_shapes=[
            pltpu.VMEM((toks, count), jnp.float32), pltpu.SemaphoreType.DMA((parts,)),
        ],
        out_shape=jax.ShapeDtypeStruct((toks, count), jnp.float32),
        compiler_params=params,
        cost_estimate=size,
    )(mine, other)
    return student, lags


def body(*args):
    seqs, blocks = lax.axis_size("dp"), lax.axis_size("ctx")

    def exchange(x):
        cut = x.reshape(seqs * blocks, -1, HALF, x.shape[1])
        got = lax.all_to_all(cut, ("dp", "ctx"), split_axis=0, concat_axis=0, tiled=True)
        return got.reshape(x.shape)

    got = exchange(filters(exchange(pack(*args)), seqs, blocks))
    partner = [(d, d + 1 - 2 * (d % 2)) for d in range(seqs)]
    return unpack(got, lambda x: lax.ppermute(x, "dp", partner))


def solution(mesh):
    placed = (
        P("dp", "ctx"),
        P(),
        P("dp", "ctx", None),
        P("dp", "ctx", None),
        P("dp", "ctx", None),
        P("ctx", None),
        P("ctx", None),
    )
    return jax.shard_map(
        body,
        mesh=mesh,
        in_specs=placed,
        out_specs=(P("dp", "ctx", None), P("ctx", None)),
        check_vma=False,
    )
```
